32 devices in a mesh: wall: 8 (over y, x, core), stream: 4 (over z).
Axes of the slice: x: 2, y: 2, z: 4, core: 2. Of those that a mesh axis runs over, the one named last changes fastest.
Arguments:
- cotangent: float32 [5, 16, 256, 1024], P(None, None, 'wall', 'stream'), may hold values from -6 to 6
- lower: float32 [5, 256], P(None, 'wall'), may hold values from 0 to 1, as said below
- pivot: float32 [5, 256], P(None, 'wall'), as said below
- speed: float32 [5, 256], P(None, 'wall'), may hold values from 0.5 to 2
Outputs:
- state_grad: float32 [5, 16, 256, 1024], P(None, None, 'wall', 'stream')
The draws below stay inside these ranges and needn't reach their ends.
Inputs may be any that keep to these rules, and one draw needn't show every extreme that they name: `lower`: every multiplier is strictly between 0 and 1. Every pivot is positive.
All inputs are finite; a program needn't handle non-finite values.
Results may differ from the reference program's by a relative error of at most 0.00012.
Values sent between devices are 32-bit elements; how exact they have to be, the bound alone decides.
A program may use at most 64 MiB of HBM per device.

```python
import math
import jax
import jax.numpy as jnp
from jax import lax

FLOW_VARIABLES = 5
PLANES = 16
CY = 32
NORMAL_ROWS = 256
NX = 1024


def decay_pair(key):
    parent_key = jax.random.fold_in(key, 17)
    sluggish_key, row_key, block_key, spike_key, trim_key = jax.random.split(parent_key, 5)
    slow_mask = jax.random.uniform(sluggish_key, (FLOW_VARIABLES,)) < 0.5
    base_rate = jnp.where(slow_mask, 0.15 / NORMAL_ROWS, 0.02)
    row_factor = jnp.exp(jax.random.uniform(row_key, (FLOW_VARIABLES, NORMAL_ROWS), minval=math.log(0.3), maxval=math.log(3.0)))
    block_factor = jnp.exp(jax.random.uniform(block_key, (FLOW_VARIABLES, NORMAL_ROWS // CY), minval=math.log(0.5), maxval=math.log(2.0)))
    rate_all = base_rate[:, None] * row_factor * jnp.repeat(block_factor, CY, axis=1)
    retain_rate = jnp.exp(-rate_all)
    spike_rows = jax.random.randint(spike_key, (FLOW_VARIABLES, 2), 0, NORMAL_ROWS)
    location_list = jnp.arange(NORMAL_ROWS)
    spike_mask = jnp.any(location_list[None, :, None] == spike_rows[:, None, :], axis=2)
    trim_factor = jax.random.uniform(trim_key, (FLOW_VARIABLES, NORMAL_ROWS), minval=0.5, maxval=0.8)
    retain_rate = jnp.where(spike_mask, retain_rate * trim_factor, retain_rate)
    return (retain_rate, base_rate)


def draw_lower(key, part):
    retain_rate, base_rate = decay_pair(key)
    return retain_rate.astype(jnp.float32)


def draw_pivot(key, part):
    retain_rate, base_rate = decay_pair(key)
    rough = jnp.exp(jax.random.uniform(jax.random.fold_in(key, 29), (FLOW_VARIABLES, NORMAL_ROWS), minval=math.log(0.5), maxval=math.log(2.0)))
    scale_field = 0.5 * (1.27 * base_rate + math.pi / NORMAL_ROWS) ** (-1.5)
    return (scale_field[:, None] * rough).astype(jnp.float32)


def block_scale(stream_key, extent, cuts, low, top_value):
    gain = 1.0
    for axis_at, shards_of in cuts:
        steps = jax.random.uniform(jax.random.fold_in(jax.random.fold_in(stream_key, 6), axis_at), (shards_of,), jnp.float32, low / len(cuts), top_value / len(cuts))
        gain = gain * jnp.repeat(jnp.exp(steps), extent[axis_at] // shards_of).reshape((-1,) + (1,) * (len(extent) - 1 - axis_at))
    return gain


def scatter_about(rng, extent, width, bound, pieces=(), kind=jnp.bfloat16):
    drawn = jax.random.normal(rng, extent, jnp.float32) * width
    if len(pieces) > 0:
        drawn = block_scale(rng, extent, pieces, -0.22, 0.18) * drawn
    return jnp.clip(drawn, min=-bound, max=bound).astype(kind)


def setup_inputs(seed: int = 0) -> dict:
    key_of = jax.random.split(jax.random.key(seed), 5)
    cotangent = scatter_about(key_of[0], (FLOW_VARIABLES, PLANES, NORMAL_ROWS, NX), 1.0, 6.0, ((2, 8), (3, 4)), jnp.float32)
    lower = draw_lower(jax.random.fold_in(key_of[4], 71), 0)
    pivot = draw_pivot(jax.random.fold_in(key_of[4], 71), 0)
    speed = jnp.clip(0.5 + 1.5 * jax.random.uniform(key_of[3], (FLOW_VARIABLES, NORMAL_ROWS), jnp.float32) ** block_scale(key_of[3], (FLOW_VARIABLES, NORMAL_ROWS), ((1, 8),), -0.2, 0.2), 0.5, 2.0)
    return dict(cotangent=cotangent, lower=lower, pivot=pivot, speed=speed)


first_coeff = 7.0 / 9.0
second_coeff = 1.0 / 36.0


def line_solve(operands):
    gradient, lower_line, pivot_line, speed_line = operands
    by_rows = jnp.moveaxis(gradient, 1, 0)
    zeros_plane = jnp.zeros(by_rows.shape[1:], by_rows.dtype)

    def up_step(carried_in, element):
        value, factor = element
        current = value + carried_in
        return factor * current, current

    _, rising = lax.scan(up_step, zeros_plane, (by_rows, lower_line))
    scaled = rising / pivot_line[:, None, None]

    def down_step(carried_in, element):
        value, factor = element
        current = value + factor * carried_in
        return current, current

    _, adjoint = lax.scan(down_step, zeros_plane, (scaled, lower_line), reverse=True)
    flux_line = speed_line[:, None, None] * adjoint
    spectrum = jnp.fft.rfft(flux_line, axis=-1)
    angles = 2.0 * math.pi * jnp.arange(NX // 2 + 1).astype(flux_line.dtype) / NX
    symbol = 2.0 * (first_coeff * jnp.sin(angles) + second_coeff * jnp.sin(2.0 * angles)) / (1.0 + (2.0 / 3.0) * jnp.cos(angles))
    derivative = jnp.fft.irfft(spectrum * (1j * symbol), n=NX, axis=-1).astype(adjoint.dtype)
    return jnp.moveaxis(adjoint + derivative, 0, 1)


def reference(cotangent, lower, pivot, speed):
    return lax.map(line_solve, (cotangent, lower, pivot, speed))
```

```python
import functools
import math

import jax
import jax.numpy as jnp
import ml_dtypes
import numpy as np
from jax import lax
from jax.experimental import pallas as pl
from jax.experimental.pallas import tpu as pltpu
from jax.sharding import PartitionSpec as P

root_value = (math.sqrt(5.0) - 3.0) / 2.0
inverse_gain = 3.0 / math.sqrt(5.0)
first_coeff = 7.0 / 9.0
second_coeff = 1.0 / 36.0
MESH = pl.DeviceIdType.MESH
VMEM_LIMIT = 40 * 1024 * 1024


def up_to(value, unit):
    return -(-value // unit) * unit


def split_np(values):
    high = values.astype(ml_dtypes.bfloat16)
    low = (values - high.astype(np.float64)).astype(ml_dtypes.bfloat16)
    return high, low


def split(values):
    high = values.astype(jnp.bfloat16)
    low = (values - high.astype(jnp.float32)).astype(jnp.bfloat16)
    return high, low


def stream_constants(length):
    r = root_value
    cell = np.arange(length)
    offset = cell[:, None] - cell[None, :]
    power = lambda d: r ** np.abs(d).astype(np.float64)
    inner = first_coeff * (power(offset - 1) - power(offset + 1))
    inner = inverse_gain * (inner + second_coeff * (power(offset - 2) - power(offset + 2)))
    kappa = inverse_gain * (first_coeff * (1 / r - r) + second_coeff * (r**-2 - r**2))
    delta = inverse_gain * second_coeff * (r - 1 / r)
    weights = np.zeros((8, length))
    weights[0] = r ** (length - 1.0 - cell)
    weights[1, length - 1] = 1.0
    weights[2] = r ** (1.0 * cell)
    weights[3, 0] = 1.0
    profile = np.zeros((8, length))
    profile[0] = -kappa * r ** (cell + 1.0)
    profile[1, 0] = -delta
    profile[2] = kappa * r ** (1.0 * length - cell)
    profile[3, length - 1] = delta
    stencil = np.concatenate(split_np(inner), axis=0)
    edges = np.concatenate(split_np(weights), axis=0)
    high, low = split_np(profile)
    profiles = np.concatenate([high, low, high, low], axis=0)
    return stencil, edges, profiles


def exchange_kernel(
    n, streams, fields, planes, rows, length, share,
    cot_hbm, low_ref, pivot_ref, speed_ref, stencil_hbm, edges_ref,
    base_hbm, from_left, from_right,
    cot, settle, base, stencil, sent, got, answer, carried, to_left, to_right,
    load_sem, stencil_sem, store_sem, send1, recv1, send2, recv2, send3, recv3,
):
    wall = lax.axis_index("wall")
    stream = lax.axis_index("stream")
    right = lax.rem(stream + 1, streams)
    left = lax.rem(stream + streams - 1, streams)

    loads = [
        pltpu.make_async_copy(cot_hbm.at[f], cot.at[f], load_sem.at[f]) for f in range(fields)
    ]
    for load in loads:
        load.start()
    stencil_load = pltpu.make_async_copy(stencil_hbm, stencil, stencil_sem)
    stencil_load.start()

    barrier = pltpu.get_barrier_semaphore()
    for d in range(1, n):
        pl.semaphore_signal(
            barrier, inc=1, device_id={"wall": lax.rem(wall + d, n)}, device_id_type=MESH
        )
    for side in (left, right):
        pl.semaphore_signal(barrier, inc=1, device_id={"stream": side}, device_id_type=MESH)

    lanes = 4 * rows
    total = fields * rows
    row_at = lax.rem(lax.broadcasted_iota(jnp.int32, (total, lanes), 0), rows)
    col_at = lax.rem(lax.broadcasted_iota(jnp.int32, (total, lanes), 1), rows)
    small_row = lax.broadcasted_iota(jnp.int32, (rows, rows), 0)
    small_col = lax.broadcasted_iota(jnp.int32, (rows, rows), 1)

    def column(ref, shift):
        pick = small_row == small_col + shift
        return jnp.concatenate(
            [
                jnp.sum(jnp.where(pick, ref[f : f + 1, :], 0.0), axis=1, keepdims=True)
                for f in range(fields)
            ],
            axis=0,
        )

    before = column(low_ref, 1)
    inverse_pivot = 1.0 / column(pivot_ref, 0)
    speed = column(speed_ref, 0)
    product = jnp.where(row_at > col_at, before, 1.0)
    step = 1
    while step < rows:
        product = product * jnp.where(row_at >= step, pltpu.roll(product, step, 0), 1.0)
        step *= 2
    factor = jnp.where(row_at >= col_at, product, 0.0)
    weighted = factor * inverse_pivot

    lane = lax.broadcasted_iota(jnp.int32, (rows, lanes), 1)
    wide_row = lax.broadcasted_iota(jnp.int32, (rows, lanes), 0)
    coeff_lane = lax.broadcasted_iota(jnp.int32, (1, length), 1)
    half = length // 2
    operators, spreads, leaves, speeds = [], [], [], []
    coeffs = jnp.zeros((1, length), jnp.float32)
    for f in range(fields):
        span = slice(f * rows, (f + 1) * rows)
        gram = lax.dot_general(
            weighted[span], factor[span], (((0,), (0,)), ((), ())),
            precision=lax.Precision.HIGHEST, preferred_element_type=jnp.float32,
        )[:rows]
        last = low_ref[f : f + 1, rows - 1 : rows]
        leave_row = factor[(f + 1) * rows - 1 : (f + 1) * rows] * last
        leave = jnp.sum(jnp.where(lane == wide_row, leave_row, 0.0), axis=1, keepdims=True)
        spread = gram[:, 0:1]
        coeffs = coeffs + jnp.where(coeff_lane == f, leave_row[:, 0:1], 0.0)
        coeffs = coeffs + jnp.where(coeff_lane == half + f, spread[0:1], 0.0)
        extra = jnp.where(wide_row[:16] == 0, leave_row, 0.0)
        stacked = jnp.concatenate([gram, extra], axis=0)
        high = stacked.astype(jnp.bfloat16).astype(jnp.float32)
        low_or_high = jnp.where(
            lax.broadcasted_iota(jnp.int32, (rows + 16, lanes), 1) < 2 * rows, high, stacked - high
        )
        operators.append(low_or_high.astype(jnp.bfloat16))
        spreads.append(jnp.broadcast_to(spread, (rows, length)))
        leaves.append(jnp.broadcast_to(leave, (rows, length)))
        speeds.append(jnp.broadcast_to(speed[span], (rows, length)))
    for o in range(n):
        depth = sent.shape[1] - 2 * share
        sent[o, 2 * share :, :] = jnp.broadcast_to(coeffs, (depth, length))

    for f in range(fields):
        loads[f].wait()
        for z in range(planes):
            line = f * planes + z
            high, low = split(cot[f, z])
            out = jnp.dot(
                operators[f],
                jnp.concatenate([high, low, high, low], axis=0),
                preferred_element_type=jnp.float32,
            )
            settle[f, z] = out[:rows]
            sent[line // share, line % share, :] = out[rows]
            sent[line // share, share + line % share, :] = out[0]

    pl.semaphore_wait(barrier, n + 1)

    def swap(source, target, send, recv, d):
        peer = lax.rem(wall + d, n)
        return pltpu.make_async_remote_copy(
            src_ref=source.at[peer], dst_ref=target.at[wall],
            send_sem=send.at[peer], recv_sem=recv.at[wall],
            device_id={"wall": peer}, device_id_type=MESH,
        )

    def arrive(source, target, send, recv, d):
        peer = lax.rem(wall + d, n)
        pltpu.make_async_remote_copy(
            src_ref=source.at[peer], dst_ref=target.at[peer],
            send_sem=send.at[peer], recv_sem=recv.at[peer],
            device_id={"wall": peer}, device_id_type=MESH,
        ).wait_recv()

    first = [swap(sent, got, send1, recv1, d) for d in range(1, n)]
    for copy in first:
        copy.start()
    got[wall] = sent[wall]
    for d in range(1, n):
        arrive(sent, got, send1, recv1, d)

    line_field = (wall * share + lax.broadcasted_iota(jnp.int32, (share, length), 0)) // planes
    share_lane = lax.broadcasted_iota(jnp.int32, (share, length), 1)
    incoming = jnp.zeros((share, length), jnp.float32)
    through, crest = [], []
    for b in range(n):
        coeff_row = got[b, 2 * share : 2 * share + 1, :]
        t = jnp.sum(jnp.where(share_lane == line_field, coeff_row, 0.0), axis=1, keepdims=True)
        p = jnp.sum(
            jnp.where(share_lane == line_field + half, coeff_row, 0.0), axis=1, keepdims=True
        )
        answer[b, 0:share, :] = incoming
        through.append(t)
        crest.append(got[b, share : 2 * share, :] + p * incoming)
        incoming = t * incoming + got[b, 0:share, :]
    descent = jnp.zeros((share, length), jnp.float32)
    pad = answer.shape[1] - 2 * share
    for b in range(n - 1, -1, -1):
        answer[b, share : 2 * share, :] = descent
        if pad:
            answer[b, 2 * share :, :] = jnp.zeros((pad, length), jnp.float32)
        descent = through[b] * descent + crest[b]

    second = [swap(answer, carried, send2, recv2, d) for d in range(1, n)]
    for copy in second:
        copy.start()
    carried[wall] = answer[wall]
    stencil_load.wait()
    for d in range(1, n):
        arrive(answer, carried, send2, recv2, d)

    edges = edges_ref[...]
    for f in range(fields):
        for z in range(planes):
            line = f * planes + z
            at = line // share, line % share
            up = carried[at[0], at[1] : at[1] + 1, :]
            down = carried[at[0], share + at[1] : share + at[1] + 1, :]
            adjoint = settle[f, z] + spreads[f] * up + leaves[f] * down
            base[f, z] = adjoint
            settle[f, z] = speeds[f] * adjoint
        high, low = split(settle[f].reshape(planes * rows, length))
        dims = (((1,), (1,)), ((), ()))
        sums = lax.dot_general(edges, high, dims, preferred_element_type=jnp.float32)
        rest = lax.dot_general(edges, low, dims, preferred_element_type=jnp.float32)
        sums = sums[:8] + sums[8:] + rest[:8]
        to_right[f] = sums[0:2]
        to_left[f] = sums[2:4]

    third = [
        pltpu.make_async_remote_copy(
            src_ref=source, dst_ref=target, send_sem=send3.at[i], recv_sem=recv3.at[i],
            device_id={"stream": side}, device_id_type=MESH,
        )
        for i, (source, target, side) in enumerate(
            ((to_right, from_left, right), (to_left, from_right, left))
        )
    ]
    for copy in third:
        copy.start()

    stores = []
    for f in range(fields):
        high, low = split(settle[f].reshape(planes * rows, length))
        slope = jnp.dot(high, stencil[:length], preferred_element_type=jnp.float32)
        slope = slope + jnp.dot(low, stencil[:length], preferred_element_type=jnp.float32)
        slope = slope + jnp.dot(high, stencil[length:], preferred_element_type=jnp.float32)
        base[f] = base[f] + slope.reshape(planes, rows, length)
        store = pltpu.make_async_copy(base.at[f], base_hbm.at[f], store_sem.at[f])
        store.start()
        stores.append(store)
    for copy in first + second:
        copy.wait_send()
    for copy in third:
        copy.wait()
    for store in stores:
        store.wait()


def halo_kernel(planes, rows, length, base_ref, left_ref, right_ref, profile_ref, out_ref):
    blank = jnp.zeros((4, planes * rows), jnp.float32)
    sums = jnp.concatenate([left_ref[0], right_ref[0], blank], axis=0)
    high = sums.astype(jnp.bfloat16).astype(jnp.float32)
    stacked = jnp.concatenate([high, high, sums - high, sums - high], axis=0).astype(jnp.bfloat16)
    halo = lax.dot_general(
        stacked, profile_ref[...], (((0,), (0,)), ((), ())), preferred_element_type=jnp.float32
    )
    out_ref[0] = base_ref[0] + halo.reshape(planes, rows, length)


def local(n, streams, cotangent, lower, pivot, speed):
    fields, planes, rows, length = cotangent.shape
    share = -(-fields * planes // n)
    stencil, edges, profiles = stream_constants(length)
    depth1 = up_to(2 * share + 1, 8)
    depth2 = up_to(2 * share, 8)
    edge_shape = (fields, 2, planes * rows)
    vmem = pl.BlockSpec(memory_space=pltpu.VMEM)
    hbm = pl.BlockSpec(memory_space=pl.ANY)
    f32 = jnp.float32
    dma = pltpu.SemaphoreType.DMA
    base, from_left, from_right = pl.pallas_call(
        functools.partial(exchange_kernel, n, streams, fields, planes, rows, length, share),
        out_shape=(
            jax.ShapeDtypeStruct(cotangent.shape, f32),
            jax.ShapeDtypeStruct(edge_shape, f32),
            jax.ShapeDtypeStruct(edge_shape, f32),
        ),
        in_specs=[hbm, vmem, vmem, vmem, hbm, vmem],
        out_specs=(hbm, vmem, vmem),
        scratch_shapes=[
            pltpu.VMEM(cotangent.shape, f32),
            pltpu.VMEM(cotangent.shape, f32),
            pltpu.VMEM(cotangent.shape, f32),
            pltpu.VMEM(stencil.shape, jnp.bfloat16),
            pltpu.VMEM((n, depth1, length), f32),
            pltpu.VMEM((n, depth1, length), f32),
            pltpu.VMEM((n, depth2, length), f32),
            pltpu.VMEM((n, depth2, length), f32),
            pltpu.VMEM(edge_shape, f32),
            pltpu.VMEM(edge_shape, f32),
            dma((fields,)),
            dma,
            dma((fields,)),
            dma((n,)),
            dma((n,)),
            dma((n,)),
            dma((n,)),
            dma((2,)),
            dma((2,)),
        ],
        compiler_params=pltpu.CompilerParams(
            collective_id=0, has_side_effects=True, vmem_limit_bytes=VMEM_LIMIT
        ),
    )(cotangent, lower, pivot, speed, jnp.asarray(stencil), jnp.asarray(edges))
    block = pl.BlockSpec((1, planes, rows, length), lambda f: (f, 0, 0, 0))
    side = pl.BlockSpec((1,) + edge_shape[1:], lambda f: (f, 0, 0))
    profile_spec = pl.BlockSpec(profiles.shape, lambda f: (0, 0))
    return pl.pallas_call(
        functools.partial(halo_kernel, planes, rows, length),
        grid=(fields,),
        out_shape=jax.ShapeDtypeStruct(cotangent.shape, f32),
        in_specs=[block, side, side, profile_spec],
        out_specs=block,
        compiler_params=pltpu.CompilerParams(vmem_limit_bytes=VMEM_LIMIT),
    )(base, from_left, from_right, jnp.asarray(profiles))


def solution(mesh):
    return jax.shard_map(
        functools.partial(local, mesh.shape["wall"], mesh.shape["stream"]),
        mesh=mesh,
        in_specs=(
            P(None, None, "wall", "stream"),
            P(None, "wall"),
            P(None, "wall"),
            P(None, "wall"),
        ),
        out_specs=P(None, None, "wall", "stream"),
        check_vma=False,
    )
```

```python
import functools
import math

import jax
import jax.numpy as jnp
from jax import lax
from jax.experimental import pallas as pl
from jax.experimental.pallas import tpu as pltpu
from jax.sharding import PartitionSpec as P

root_value = (math.sqrt(5.0) - 3.0) / 2.0
inverse_gain = 3.0 / math.sqrt(5.0)
first_coeff = 7.0 / 9.0
second_coeff = 1.0 / 36.0
MESH = pl.DeviceIdType.MESH
VMEM_LIMIT = 40 * 1024 * 1024


def up_to(value, unit):
    return -(-value // unit) * unit


def split(values):
    high = values.astype(jnp.bfloat16)
    low = (values - high.astype(jnp.float32)).astype(jnp.bfloat16)
    return high, low


def root_power(steps):
    even = steps - 2.0 * jnp.floor(steps * 0.5) == 0.0
    size = jnp.exp(steps * math.log(-root_value))
    return jnp.where(even, size, -size)


far_scale = inverse_gain * (
    first_coeff * (1.0 / root_value - root_value)
    + second_coeff * (root_value**-2 - root_value**2)
)
near_shift = inverse_gain * second_coeff * (root_value - 1.0 / root_value)


def stencil_block(length):
    source = lax.broadcasted_iota(jnp.int32, (length, length), 0)
    target = lax.broadcasted_iota(jnp.int32, (length, length), 1)
    offset = source - target
    steps = jnp.abs(offset).astype(jnp.float32)
    size = far_scale * root_power(steps) + jnp.where(steps == 1.0, near_shift, 0.0)
    return jnp.where(offset > 0, size, jnp.where(offset < 0, -size, 0.0))


def edge_weights(length):
    row = lax.broadcasted_iota(jnp.int32, (8, length), 0)
    cell = lax.broadcasted_iota(jnp.int32, (8, length), 1)
    back = length - 1 - cell
    decay = root_power(jnp.where(row == 0, back, cell).astype(jnp.float32))
    edge = jnp.where(jnp.where(row == 1, back, cell) == 0, 1.0, 0.0)
    weights = jnp.where((row == 0) | (row == 2), decay, edge)
    return jnp.where(row < 4, weights, 0.0)


def edge_profiles(length):
    row = lax.broadcasted_iota(jnp.int32, (8, length), 0)
    cell = lax.broadcasted_iota(jnp.int32, (8, length), 1)
    back = length - 1 - cell
    depth = jnp.where(row < 2, cell, back)
    decay = far_scale * root_power((depth + 1).astype(jnp.float32))
    edge = jnp.where(depth == 0, near_shift, 0.0)
    profile = jnp.where((row == 0) | (row == 2), decay, edge)
    return jnp.where(row < 2, -profile, jnp.where(row < 4, profile, 0.0))


def exchange_kernel(
    n, streams, fields, planes, rows, length, share,
    cot_hbm, low_hbm, pivot_hbm, speed_hbm,
    base, from_left, from_right,
    cot, settle, low_ref, pivot_ref, speed_ref, sent, got, answer, carried, to_left, to_right,
    load_sem, row_sem, send1, recv1, send2, recv2, send3, recv3,
):
    wall = lax.axis_index("wall")
    stream = lax.axis_index("stream")
    right = lax.rem(stream + 1, streams)
    left = lax.rem(stream + streams - 1, streams)

    row_loads = [
        pltpu.make_async_copy(source, target, row_sem.at[i])
        for i, (source, target) in enumerate(
            ((low_hbm, low_ref), (pivot_hbm, pivot_ref), (speed_hbm, speed_ref))
        )
    ]
    for load in row_loads:
        load.start()
    loads = [
        pltpu.make_async_copy(cot_hbm.at[f], cot.at[f], load_sem.at[f]) for f in range(fields)
    ]
    for load in loads:
        load.start()

    barrier = pltpu.get_barrier_semaphore()
    for d in range(1, n):
        pl.semaphore_signal(
            barrier, inc=1, device_id={"wall": lax.rem(wall + d, n)}, device_id_type=MESH
        )
    for side in (left, right):
        pl.semaphore_signal(barrier, inc=1, device_id={"stream": side}, device_id_type=MESH)

    lanes = 4 * rows
    total = fields * rows
    row_at = lax.rem(lax.broadcasted_iota(jnp.int32, (total, lanes), 0), rows)
    col_at = lax.rem(lax.broadcasted_iota(jnp.int32, (total, lanes), 1), rows)
    small_row = lax.broadcasted_iota(jnp.int32, (rows, rows), 0)
    small_col = lax.broadcasted_iota(jnp.int32, (rows, rows), 1)

    def column(ref, shift):
        pick = small_row == small_col + shift
        return jnp.concatenate(
            [
                jnp.sum(jnp.where(pick, ref[f : f + 1, :], 0.0), axis=1, keepdims=True)
                for f in range(fields)
            ],
            axis=0,
        )

    for load in row_loads:
        load.wait()
    before = column(low_ref, 1)
    inverse_pivot = 1.0 / column(pivot_ref, 0)
    speed = column(speed_ref, 0)
    product = jnp.where(row_at > col_at, before, 1.0)
    step = 1
    while step < rows:
        product = product * jnp.where(row_at >= step, pltpu.roll(product, step, 0), 1.0)
        step *= 2
    factor = jnp.where(row_at >= col_at, product, 0.0)
    weighted = factor * inverse_pivot

    lane = lax.broadcasted_iota(jnp.int32, (rows, lanes), 1)
    wide_row = lax.broadcasted_iota(jnp.int32, (rows, lanes), 0)
    coeff_lane = lax.broadcasted_iota(jnp.int32, (1, length), 1)
    half = length // 2
    operators, spreads, leaves, speeds = [], [], [], []
    coeffs = jnp.zeros((1, length), jnp.float32)
    for f in range(fields):
        span = slice(f * rows, (f + 1) * rows)
        gram = lax.dot_general(
            weighted[span], factor[span], (((0,), (0,)), ((), ())),
            precision=lax.Precision.HIGHEST, preferred_element_type=jnp.float32,
        )[:rows]
        last = low_ref[f : f + 1, rows - 1 : rows]
        leave_row = factor[(f + 1) * rows - 1 : (f + 1) * rows] * last
        leave = jnp.sum(jnp.where(lane == wide_row, leave_row, 0.0), axis=1, keepdims=True)
        spread = gram[:, 0:1]
        coeffs = coeffs + jnp.where(coeff_lane == f, leave_row[:, 0:1], 0.0)
        coeffs = coeffs + jnp.where(coeff_lane == half + f, spread[0:1], 0.0)
        extra = jnp.where(wide_row[:16] == 0, leave_row, 0.0)
        stacked = jnp.concatenate([gram, extra], axis=0)
        high = stacked.astype(jnp.bfloat16).astype(jnp.float32)
        low_or_high = jnp.where(
            lax.broadcasted_iota(jnp.int32, (rows + 16, lanes), 1) < 2 * rows, high, stacked - high
        )
        operators.append(low_or_high.astype(jnp.bfloat16))
        spreads.append(jnp.broadcast_to(spread, (rows, length)))
        leaves.append(jnp.broadcast_to(leave, (rows, length)))
        speeds.append(jnp.broadcast_to(speed[span], (rows, length)))
    for o in range(n):
        depth = sent.shape[1] - 2 * share
        sent[o, 2 * share :, :] = jnp.broadcast_to(coeffs, (depth, length))

    for f in range(fields):
        loads[f].wait()
        for z in range(planes):
            line = f * planes + z
            high, low = split(cot[f, z])
            out = jnp.dot(
                operators[f],
                jnp.concatenate([high, low, high, low], axis=0),
                preferred_element_type=jnp.float32,
            )
            settle[f, z] = out[:rows]
            sent[line // share, line % share, :] = out[rows]
            sent[line // share, share + line % share, :] = out[0]

    pl.semaphore_wait(barrier, n + 1)

    def swap(source, target, send, recv, d):
        peer = lax.rem(wall + d, n)
        return pltpu.make_async_remote_copy(
            src_ref=source.at[peer], dst_ref=target.at[wall],
            send_sem=send.at[peer], recv_sem=recv.at[wall],
            device_id={"wall": peer}, device_id_type=MESH,
        )

    def arrive(source, target, send, recv, d):
        peer = lax.rem(wall + d, n)
        pltpu.make_async_remote_copy(
            src_ref=source.at[peer], dst_ref=target.at[peer],
            send_sem=send.at[peer], recv_sem=recv.at[peer],
            device_id={"wall": peer}, device_id_type=MESH,
        ).wait_recv()

    first = [swap(sent, got, send1, recv1, d) for d in range(1, n)]
    for copy in first:
        copy.start()
    got[wall] = sent[wall]
    for d in range(1, n):
        arrive(sent, got, send1, recv1, d)

    line_field = (wall * share + lax.broadcasted_iota(jnp.int32, (share, length), 0)) // planes
    share_lane = lax.broadcasted_iota(jnp.int32, (share, length), 1)
    incoming = jnp.zeros((share, length), jnp.float32)
    through, crest = [], []
    for b in range(n):
        coeff_row = got[b, 2 * share : 2 * share + 1, :]
        t = jnp.sum(jnp.where(share_lane == line_field, coeff_row, 0.0), axis=1, keepdims=True)
        p = jnp.sum(
            jnp.where(share_lane == line_field + half, coeff_row, 0.0), axis=1, keepdims=True
        )
        answer[b, 0:share, :] = incoming
        through.append(t)
        crest.append(got[b, share : 2 * share, :] + p * incoming)
        incoming = t * incoming + got[b, 0:share, :]
    descent = jnp.zeros((share, length), jnp.float32)
    pad = answer.shape[1] - 2 * share
    for b in range(n - 1, -1, -1):
        answer[b, share : 2 * share, :] = descent
        if pad:
            answer[b, 2 * share :, :] = jnp.zeros((pad, length), jnp.float32)
        descent = through[b] * descent + crest[b]

    second = [swap(answer, carried, send2, recv2, d) for d in range(1, n)]
    for copy in second:
        copy.start()
    carried[wall] = answer[wall]
    stencil_high, stencil_low = split(stencil_block(length))
    weights = edge_weights(length)
    high = weights.astype(jnp.bfloat16).astype(jnp.float32)
    edges = jnp.concatenate([high, weights - high], axis=0).astype(jnp.bfloat16)
    for d in range(1, n):
        arrive(answer, carried, send2, recv2, d)

    for f in range(fields):
        for z in range(planes):
            line = f * planes + z
            at = line // share, line % share
            up = carried[at[0], at[1] : at[1] + 1, :]
            down = carried[at[0], share + at[1] : share + at[1] + 1, :]
            adjoint = settle[f, z] + spreads[f] * up + leaves[f] * down
            base[f, z] = adjoint
            settle[f, z] = speeds[f] * adjoint
        high, low = split(settle[f].reshape(planes * rows, length))
        dims = (((1,), (1,)), ((), ()))
        sums = lax.dot_general(edges, high, dims, preferred_element_type=jnp.float32)
        rest = lax.dot_general(edges, low, dims, preferred_element_type=jnp.float32)
        sums = sums[:8] + sums[8:] + rest[:8]
        to_right[f] = sums[0:2]
        to_left[f] = sums[2:4]

    third = [
        pltpu.make_async_remote_copy(
            src_ref=source, dst_ref=target, send_sem=send3.at[i], recv_sem=recv3.at[i],
            device_id={"stream": side}, device_id_type=MESH,
        )
        for i, (source, target, side) in enumerate(
            ((to_right, from_left, right), (to_left, from_right, left))
        )
    ]
    for copy in third:
        copy.start()

    for f in range(fields):
        high, low = split(settle[f].reshape(planes * rows, length))
        slope = jnp.dot(high, stencil_high, preferred_element_type=jnp.float32)
        slope = slope + jnp.dot(low, stencil_high, preferred_element_type=jnp.float32)
        slope = slope + jnp.dot(high, stencil_low, preferred_element_type=jnp.float32)
        base[f] = base[f] + slope.reshape(planes, rows, length)
    for copy in first + second:
        copy.wait_send()
    for copy in third:
        copy.wait()


def halo_kernel(
    fields, planes, rows, length, base, from_left, from_right, out_hbm, out, store_sem
):
    profile = edge_profiles(length)
    high = profile.astype(jnp.bfloat16).astype(jnp.float32)
    profiles = jnp.concatenate([high, profile - high, high, profile - high], axis=0)
    profiles = profiles.astype(jnp.bfloat16)
    blank = jnp.zeros((4, planes * rows), jnp.float32)
    stores = []
    for f in range(fields):
        sums = jnp.concatenate([from_left[f], from_right[f], blank], axis=0)
        high = sums.astype(jnp.bfloat16).astype(jnp.float32)
        rest = sums - high
        stacked = jnp.concatenate([high, high, rest, rest], axis=0).astype(jnp.bfloat16)
        halo = lax.dot_general(
            stacked, profiles, (((0,), (0,)), ((), ())), preferred_element_type=jnp.float32
        )
        out[f] = base[f] + halo.reshape(planes, rows, length)
        store = pltpu.make_async_copy(out.at[f], out_hbm.at[f], store_sem.at[f])
        store.start()
        stores.append(store)
    for store in stores:
        store.wait()


def local(n, streams, cotangent, lower, pivot, speed):
    fields, planes, rows, length = cotangent.shape
    share = -(-fields * planes // n)
    depth1 = up_to(2 * share + 1, 8)
    depth2 = up_to(2 * share, 8)
    edge_shape = (fields, 2, planes * rows)
    vmem = pl.BlockSpec(memory_space=pltpu.VMEM)
    hbm = pl.BlockSpec(memory_space=pltpu.HBM)
    f32 = jnp.float32
    dma = pltpu.SemaphoreType.DMA
    base, from_left, from_right = pl.pallas_call(
        functools.partial(exchange_kernel, n, streams, fields, planes, rows, length, share),
        out_shape=(
            jax.ShapeDtypeStruct(cotangent.shape, f32),
            jax.ShapeDtypeStruct(edge_shape, f32),
            jax.ShapeDtypeStruct(edge_shape, f32),
        ),
        in_specs=[hbm] * 4,
        out_specs=(vmem, vmem, vmem),
        scratch_shapes=[
            pltpu.VMEM(cotangent.shape, f32),
            pltpu.VMEM(cotangent.shape, f32),
            pltpu.VMEM(lower.shape, f32),
            pltpu.VMEM(lower.shape, f32),
            pltpu.VMEM(lower.shape, f32),
            pltpu.VMEM((n, depth1, length), f32),
            pltpu.VMEM((n, depth1, length), f32),
            pltpu.VMEM((n, depth2, length), f32),
            pltpu.VMEM((n, depth2, length), f32),
            pltpu.VMEM(edge_shape, f32),
            pltpu.VMEM(edge_shape, f32),
            dma((fields,)),
            dma((3,)),
            dma((n,)),
            dma((n,)),
            dma((n,)),
            dma((n,)),
            dma((2,)),
            dma((2,)),
        ],
        compiler_params=pltpu.CompilerParams(
            collective_id=0, has_side_effects=True, vmem_limit_bytes=VMEM_LIMIT
        ),
    )(*[pltpu.with_memory_space_constraint(a, pltpu.HBM) for a in (cotangent, lower, pivot, speed)])
    return pl.pallas_call(
        functools.partial(halo_kernel, fields, planes, rows, length),
        out_shape=jax.ShapeDtypeStruct(cotangent.shape, f32),
        in_specs=[vmem] * 3,
        out_specs=hbm,
        scratch_shapes=[pltpu.VMEM(cotangent.shape, f32), dma((fields,))],
        compiler_params=pltpu.CompilerParams(vmem_limit_bytes=VMEM_LIMIT),
    )(base, from_left, from_right)


def solution(mesh):
    return jax.shard_map(
        functools.partial(local, mesh.shape["wall"], mesh.shape["stream"]),
        mesh=mesh,
        in_specs=(
            P(None, None, "wall", "stream"),
            P(None, "wall"),
            P(None, "wall"),
            P(None, "wall"),
        ),
        out_specs=P(None, None, "wall", "stream"),
        check_vma=False,
    )
```

```python
import functools
import math

import jax
import jax.numpy as jnp
from jax import lax
from jax.experimental import pallas as pl
from jax.experimental.pallas import tpu as pltpu
from jax.sharding import PartitionSpec as P

root_value = (math.sqrt(5.0) - 3.0) / 2.0
inverse_gain = 3.0 / math.sqrt(5.0)
first_coeff = 7.0 / 9.0
second_coeff = 1.0 / 36.0
MESH = pl.DeviceIdType.MESH
VMEM_LIMIT = 40 * 1024 * 1024


def up_to(value, unit):
    return -(-value // unit) * unit


def split(values):
    high = values.astype(jnp.bfloat16)
    low = (values - high.astype(jnp.float32)).astype(jnp.bfloat16)
    return high, low


def root_power(steps):
    even = steps - 2.0 * jnp.floor(steps * 0.5) == 0.0
    size = jnp.exp(steps * math.log(-root_value))
    return jnp.where(even, size, -size)


far_scale = inverse_gain * (
    first_coeff * (1.0 / root_value - root_value)
    + second_coeff * (root_value**-2 - root_value**2)
)
near_shift = inverse_gain * second_coeff * (root_value - 1.0 / root_value)


def stencil_block(length):
    source = lax.broadcasted_iota(jnp.int32, (length, length), 0)
    target = lax.broadcasted_iota(jnp.int32, (length, length), 1)
    offset = source - target
    steps = jnp.abs(offset).astype(jnp.float32)
    size = far_scale * root_power(steps) + jnp.where(steps == 1.0, near_shift, 0.0)
    return jnp.where(offset > 0, size, jnp.where(offset < 0, -size, 0.0))


def edge_weights(length):
    row = lax.broadcasted_iota(jnp.int32, (8, length), 0)
    cell = lax.broadcasted_iota(jnp.int32, (8, length), 1)
    back = length - 1 - cell
    decay = root_power(jnp.where(row == 0, back, cell).astype(jnp.float32))
    edge = jnp.where(jnp.where(row == 1, back, cell) == 0, 1.0, 0.0)
    weights = jnp.where((row == 0) | (row == 2), decay, edge)
    return jnp.where(row < 4, weights, 0.0)


def edge_profiles(length):
    row = lax.broadcasted_iota(jnp.int32, (8, length), 0)
    cell = lax.broadcasted_iota(jnp.int32, (8, length), 1)
    back = length - 1 - cell
    depth = jnp.where(row < 2, cell, back)
    decay = far_scale * root_power((depth + 1).astype(jnp.float32))
    edge = jnp.where(depth == 0, near_shift, 0.0)
    profile = jnp.where((row == 0) | (row == 2), decay, edge)
    return jnp.where(row < 2, -profile, jnp.where(row < 4, profile, 0.0))


def stacked_high(values):
    high = values.astype(jnp.bfloat16).astype(jnp.float32)
    rest = values - high
    return jnp.concatenate([high, high, rest, rest], axis=0).astype(jnp.bfloat16)


def stacked_both(values):
    high = values.astype(jnp.bfloat16).astype(jnp.float32)
    rest = values - high
    return jnp.concatenate([high, rest, high, rest], axis=0).astype(jnp.bfloat16)


def down(left, right):
    return lax.dot_general(
        left, right, (((0,), (0,)), ((), ())), preferred_element_type=jnp.float32
    )


def edge_sums(edges, values):
    high, low = split(values)
    dims = (((1,), (1,)), ((), ()))
    sums = lax.dot_general(edges, high, dims, preferred_element_type=jnp.float32)
    rest = lax.dot_general(edges, low, dims, preferred_element_type=jnp.float32)
    return sums[:8] + sums[8:] + rest[:8]


def through_stencil(values, stencil):
    high, low = split(values)
    slope = jnp.dot(high, stencil[0], preferred_element_type=jnp.float32)
    slope = slope + jnp.dot(low, stencil[0], preferred_element_type=jnp.float32)
    return slope + jnp.dot(high, stencil[1], preferred_element_type=jnp.float32)


def exchange_kernel(
    n, streams, fields, planes, rows, length, share, depth, wide,
    cot_hbm, low_hbm, pivot_hbm, speed_hbm,
    base, carried_out, slope_out, columns,
    cot, low_ref, pivot_ref, speed_ref, sent, got, answer, carried,
    lines_left, lines_right, lines_from_left, lines_from_right, ends, ends_got,
    to_left, to_right, from_left, from_right,
    load_sem, row_sem, send1, recv1, send2, recv2, send3, recv3, send4, recv4, send5, recv5,
):
    wall = lax.axis_index("wall")
    stream = lax.axis_index("stream")
    right = lax.rem(stream + 1, streams)
    left = lax.rem(stream + streams - 1, streams)

    row_loads = [
        pltpu.make_async_copy(source, target, row_sem.at[i])
        for i, (source, target) in enumerate(
            ((low_hbm, low_ref), (pivot_hbm, pivot_ref), (speed_hbm, speed_ref))
        )
    ]
    for load in row_loads:
        load.start()
    loads = [
        pltpu.make_async_copy(cot_hbm.at[f], cot.at[f], load_sem.at[f]) for f in range(fields)
    ]
    for load in loads:
        load.start()

    barrier = pltpu.get_barrier_semaphore()
    for d in range(1, n):
        pl.semaphore_signal(
            barrier, inc=1, device_id={"wall": lax.rem(wall + d, n)}, device_id_type=MESH
        )
    for side in (left, right):
        pl.semaphore_signal(barrier, inc=1, device_id={"stream": side}, device_id_type=MESH)

    def swap(source, target, send, recv, d):
        peer = lax.rem(wall + d, n)
        return pltpu.make_async_remote_copy(
            src_ref=source.at[peer], dst_ref=target.at[wall],
            send_sem=send.at[peer], recv_sem=recv.at[wall],
            device_id={"wall": peer}, device_id_type=MESH,
        )

    def arrive(source, target, send, recv, d):
        peer = lax.rem(wall + d, n)
        pltpu.make_async_remote_copy(
            src_ref=source.at[peer], dst_ref=target.at[peer],
            send_sem=send.at[peer], recv_sem=recv.at[peer],
            device_id={"wall": peer}, device_id_type=MESH,
        ).wait_recv()

    def beside(pairs, send, recv):
        return [
            pltpu.make_async_remote_copy(
                src_ref=source, dst_ref=target, send_sem=send.at[i], recv_sem=recv.at[i],
                device_id={"stream": side}, device_id_type=MESH,
            )
            for i, (source, target, side) in enumerate(pairs)
        ]

    sent[...] = jnp.zeros(sent.shape, jnp.float32)
    weights = edge_weights(length)
    high = weights.astype(jnp.bfloat16).astype(jnp.float32)
    edges = jnp.concatenate([high, weights - high], axis=0).astype(jnp.bfloat16)

    lanes = 4 * rows
    total = fields * rows
    row_at = lax.rem(lax.broadcasted_iota(jnp.int32, (total, lanes), 0), rows)
    col_at = lax.rem(lax.broadcasted_iota(jnp.int32, (total, lanes), 1), rows)
    small_row = lax.broadcasted_iota(jnp.int32, (rows, rows), 0)
    small_col = lax.broadcasted_iota(jnp.int32, (rows, rows), 1)

    def column(ref, shift):
        pick = small_row == small_col + shift
        return jnp.concatenate(
            [
                jnp.sum(jnp.where(pick, ref[f : f + 1, :], 0.0), axis=1, keepdims=True)
                for f in range(fields)
            ],
            axis=0,
        )

    for load in row_loads:
        load.wait()
    before = column(low_ref, 1)
    inverse_pivot = 1.0 / column(pivot_ref, 0)
    speed = column(speed_ref, 0)
    product = jnp.where(row_at > col_at, before, 1.0)
    step = 1
    while step < rows:
        product = product * jnp.where(row_at >= step, pltpu.roll(product, step, 0), 1.0)
        step *= 2
    factor = jnp.where(row_at >= col_at, product, 0.0)
    weighted = factor * inverse_pivot

    lane = lax.broadcasted_iota(jnp.int32, (rows, lanes), 1)
    wide_row = lax.broadcasted_iota(jnp.int32, (rows, lanes), 0)
    coeff_lane = lax.broadcasted_iota(jnp.int32, (1, length), 1)
    line_lane = lax.broadcasted_iota(jnp.int32, (1, wide), 1)
    line_index = (line_lane // depth) * share + line_lane % depth
    line_used = (line_lane % depth < share) & (line_index < fields * planes)
    line_field = jnp.where(line_used, line_index // planes, -1)
    half = length // 2
    spreads, leaves, speeds = [], [], []
    coeffs = jnp.zeros((1, length), jnp.float32)
    line_through = jnp.zeros((1, wide), jnp.float32)
    line_first = jnp.zeros((1, wide), jnp.float32)
    for f in range(fields):
        span = slice(f * rows, (f + 1) * rows)
        last = low_ref[f : f + 1, rows - 1 : rows]
        leave_row = factor[(f + 1) * rows - 1 : (f + 1) * rows] * last
        spread_row = jnp.sum(weighted[span] * factor[span, 0:1], axis=0, keepdims=True)
        leave = jnp.sum(jnp.where(lane == wide_row, leave_row, 0.0), axis=1, keepdims=True)
        spread = jnp.sum(jnp.where(lane == wide_row, spread_row, 0.0), axis=1, keepdims=True)
        coeffs = coeffs + jnp.where(coeff_lane == f, leave_row[:, 0:1], 0.0)
        coeffs = coeffs + jnp.where(coeff_lane == half + f, spread_row[:, 0:1], 0.0)
        line_through = line_through + jnp.where(line_field == f, leave_row[:, 0:1], 0.0)
        line_first = line_first + jnp.where(line_field == f, spread_row[:, 0:1], 0.0)
        spreads.append(jnp.broadcast_to(spread, (rows, length)))
        leaves.append(jnp.broadcast_to(leave, (rows, length)))
        speeds.append(jnp.broadcast_to(speed[span], (rows, length)))
        columns[0, f] = spreads[f][:, :128]
        columns[1, f] = leaves[f][:, :128]
        columns[2, f] = spreads[f][:, :128] * speeds[f][:, :128]
        columns[3, f] = leaves[f][:, :128] * speeds[f][:, :128]
    for o in range(n):
        sent[o, 2 * share : 2 * share + 1, :] = coeffs

    for f in range(fields):
        loads[f].wait()
        for z in range(planes):
            line = f * planes + z
            values = cot[f, z]
            sent[line // share, line % share, :] = jnp.sum(values * leaves[f], axis=0)
            sent[line // share, share + line % share, :] = jnp.sum(values * spreads[f], axis=0)

    pl.semaphore_wait(barrier, n + 1)

    first = [swap(sent, got, send1, recv1, d) for d in range(1, n)]
    for copy in first:
        copy.start()
    got[wall] = sent[wall]

    flat = sent[...].reshape(n * depth, length)
    if wide > n * depth:
        flat = jnp.concatenate(
            [flat, jnp.zeros((wide - n * depth, length), jnp.float32)], axis=0
        )
    sums = edge_sums(edges, flat)
    lines_right[...] = sums[0:2]
    lines_left[...] = sums[2:4]
    lines_copies = beside(
        ((lines_right, lines_from_left, right), (lines_left, lines_from_right, left)), send3, recv3
    )
    for copy in lines_copies:
        copy.start()

    def settle_field(f):
        span = slice(f * rows, (f + 1) * rows)
        gram = lax.dot_general(
            weighted[span], factor[span], (((0,), (0,)), ((), ())),
            precision=lax.Precision.HIGHEST, preferred_element_type=jnp.float32,
        )[:rows]
        high = gram.astype(jnp.bfloat16).astype(jnp.float32)
        operator = jnp.where(lane < 2 * rows, high, gram - high).astype(jnp.bfloat16)
        for z in range(planes):
            high, low = split(cot[f, z])
            out = jnp.dot(
                operator,
                jnp.concatenate([high, low, high, low], axis=0),
                preferred_element_type=jnp.float32,
            )
            base[f, z] = out
            cot[f, z] = speeds[f] * out
        sums = edge_sums(edges, cot[f].reshape(planes * rows, length))
        to_right[f] = sums[0:2]
        to_left[f] = sums[2:4]

    early = (fields + 1) // 2
    for f in range(early):
        settle_field(f)

    for copy in lines_copies:
        copy.wait_recv()
    ends[0:2, :] = lines_from_left[...]
    ends[2:4, :] = lines_from_right[...]
    ends[4:5, :] = line_through
    ends[5:6, :] = line_first
    ends[6:8, :] = jnp.zeros((2, wide), jnp.float32)
    gather = [
        pltpu.make_async_remote_copy(
            src_ref=ends, dst_ref=ends_got.at[wall],
            send_sem=send4.at[lax.rem(wall + d, n)], recv_sem=recv4.at[wall],
            device_id={"wall": lax.rem(wall + d, n)}, device_id_type=MESH,
        )
        for d in range(1, n)
    ]
    for copy in gather:
        copy.start()
    ends_got[wall] = ends[...]

    for f in range(early, fields):
        settle_field(f)
    edge_copies = beside(
        ((to_right, from_left, right), (to_left, from_right, left)), send5, recv5
    )
    for copy in edge_copies:
        copy.start()

    for d in range(1, n):
        arrive(sent, got, send1, recv1, d)

    share_field = (wall * share + lax.broadcasted_iota(jnp.int32, (share, length), 0)) // planes
    share_lane = lax.broadcasted_iota(jnp.int32, (share, length), 1)
    incoming = jnp.zeros((share, length), jnp.float32)
    through, crest = [], []
    for b in range(n):
        coeff_row = got[b, 2 * share : 2 * share + 1, :]
        t = jnp.sum(jnp.where(share_lane == share_field, coeff_row, 0.0), axis=1, keepdims=True)
        p = jnp.sum(
            jnp.where(share_lane == share_field + half, coeff_row, 0.0), axis=1, keepdims=True
        )
        answer[b, 0:share, :] = incoming
        through.append(t)
        crest.append(got[b, share : 2 * share, :] + p * incoming)
        incoming = t * incoming + got[b, 0:share, :]
    descent = jnp.zeros((share, length), jnp.float32)
    for b in range(n - 1, -1, -1):
        answer[b, share : 2 * share, :] = descent
        answer[b, 2 * share :, :] = jnp.zeros((depth - 2 * share, length), jnp.float32)
        descent = through[b] * descent + crest[b]

    second = [swap(answer, carried, send2, recv2, d) for d in range(1, n)]
    for copy in second:
        copy.start()
    carried[wall] = answer[wall]

    stencil = split(stencil_block(length))
    profiles = stacked_both(edge_profiles(length))
    blank = jnp.zeros((4, planes * rows), jnp.float32)
    for copy in edge_copies:
        copy.wait_recv()
    for f in range(fields):
        slope = through_stencil(cot[f].reshape(planes * rows, length), stencil)
        sides = jnp.concatenate([from_left[f], from_right[f], blank], axis=0)
        slope = slope + down(stacked_high(sides), profiles)
        base[f] = base[f] + slope.reshape(planes, rows, length)

    for d in range(1, n):
        peer = lax.rem(wall + d, n)
        pltpu.make_async_remote_copy(
            src_ref=ends, dst_ref=ends_got.at[peer],
            send_sem=send4.at[peer], recv_sem=recv4.at[peer],
            device_id={"wall": peer}, device_id_type=MESH,
        ).wait_recv()
    zero = jnp.zeros((8, wide), jnp.float32)
    incoming, taken_up, through, crest = zero, zero, [], []
    for b in range(n):
        arrived = ends_got[b]
        t, p = arrived[4:5], arrived[5:6]
        taken_up = jnp.where(wall == b, incoming, taken_up)
        through.append(t)
        crest.append(pltpu.roll(arrived, wide - share, 1) + p * incoming)
        incoming = t * incoming + arrived
    descent, taken_down = zero, zero
    for b in range(n - 1, -1, -1):
        taken_down = jnp.where(wall == b, descent, taken_down)
        descent = through[b] * descent + crest[b]
    side_rows = lax.broadcasted_iota(jnp.int32, (8, wide), 0) < 4
    used = side_rows & line_used
    taken_up = jnp.where(used, taken_up, 0.0)
    taken_down = jnp.where(used, taken_down, 0.0)
    halo = down(stacked_high(taken_up + pltpu.roll(taken_down, share, 1)), profiles)

    for d in range(1, n):
        arrive(answer, carried, send2, recv2, d)
    flat = carried[...].reshape(n * depth, length)
    slope = through_stencil(flat, stencil) + halo[: n * depth]
    carried_out[...] = carried[...]
    slope_out[...] = slope.reshape(n, depth, length)

    for copy in first + second + lines_copies + gather + edge_copies:
        copy.wait_send()


def gather_kernel(
    fields, planes, rows, length, share, base, carried, slopes, columns, out_hbm, out, store_sem
):
    stores = []
    for f in range(fields):
        spread, leave, spread_speed, leave_speed = (
            jnp.concatenate([columns[i, f]] * (length // 128), axis=1) for i in range(4)
        )
        for z in range(planes):
            line = f * planes + z
            o, up = line // share, line % share
            low = share + up
            value = base[f, z] + spread * carried[o, up : up + 1, :]
            value = value + leave * carried[o, low : low + 1, :]
            value = value + spread_speed * slopes[o, up : up + 1, :]
            out[f, z] = value + leave_speed * slopes[o, low : low + 1, :]
        store = pltpu.make_async_copy(out.at[f], out_hbm.at[f], store_sem.at[f])
        store.start()
        stores.append(store)
    for store in stores:
        store.wait()


def local(n, streams, cotangent, lower, pivot, speed):
    fields, planes, rows, length = cotangent.shape
    share = -(-fields * planes // n)
    depth = up_to(2 * share + 1, 8)
    wide = up_to(n * depth, 128)
    edge_shape = (fields, 2, planes * rows)
    line_shape = (n, depth, length)
    column_shape = (4, fields, rows, 128)
    vmem = pl.BlockSpec(memory_space=pltpu.VMEM)
    hbm = pl.BlockSpec(memory_space=pltpu.HBM)
    f32 = jnp.float32
    dma = pltpu.SemaphoreType.DMA
    scratch = lambda shape: pltpu.VMEM(shape, f32)
    out_shapes = (cotangent.shape, line_shape, line_shape, column_shape)
    parts = pl.pallas_call(
        functools.partial(
            exchange_kernel, n, streams, fields, planes, rows, length, share, depth, wide
        ),
        out_shape=tuple(jax.ShapeDtypeStruct(shape, f32) for shape in out_shapes),
        in_specs=[hbm] * 4,
        out_specs=(vmem,) * 4,
        scratch_shapes=[scratch(cotangent.shape)]
        + [scratch(lower.shape)] * 3
        + [scratch(line_shape)] * 4
        + [scratch((2, wide))] * 4
        + [scratch((8, wide)), scratch((n, 8, wide))]
        + [scratch(edge_shape)] * 4
        + [dma((fields,)), dma((3,))]
        + [dma((n,))] * 4
        + [dma((2,))] * 2
        + [dma((n,))] * 2
        + [dma((2,))] * 2,
        compiler_params=pltpu.CompilerParams(
            collective_id=0, has_side_effects=True, vmem_limit_bytes=VMEM_LIMIT
        ),
    )(*[
        pltpu.with_memory_space_constraint(a, pltpu.HBM)
        for a in (cotangent, lower, pivot, speed)
    ])
    return pl.pallas_call(
        functools.partial(gather_kernel, fields, planes, rows, length, share),
        out_shape=jax.ShapeDtypeStruct(cotangent.shape, f32),
        in_specs=[vmem] * 4,
        out_specs=hbm,
        scratch_shapes=[scratch(cotangent.shape), dma((fields,))],
        compiler_params=pltpu.CompilerParams(vmem_limit_bytes=VMEM_LIMIT),
    )(*parts)


def solution(mesh):
    return jax.shard_map(
        functools.partial(local, mesh.shape["wall"], mesh.shape["stream"]),
        mesh=mesh,
        in_specs=(
            P(None, None, "wall", "stream"),
            P(None, "wall"),
            P(None, "wall"),
            P(None, "wall"),
        ),
        out_specs=P(None, None, "wall", "stream"),
        check_vma=False,
    )
```

```python
import functools
import math

import jax
import jax.numpy as jnp
from jax import lax
from jax.experimental import pallas as pl
from jax.experimental.pallas import tpu as pltpu
from jax.sharding import PartitionSpec as P

root_value = (math.sqrt(5.0) - 3.0) / 2.0
inverse_gain = 3.0 / math.sqrt(5.0)
first_coeff = 7.0 / 9.0
second_coeff = 1.0 / 36.0
MESH = pl.DeviceIdType.MESH
VMEM_LIMIT = 40 * 1024 * 1024


def up_to(value, unit):
    return -(-value // unit) * unit


def split(values):
    high = values.astype(jnp.bfloat16)
    low = (values - high.astype(jnp.float32)).astype(jnp.bfloat16)
    return high, low


def root_power(steps):
    even = steps - 2.0 * jnp.floor(steps * 0.5) == 0.0
    size = jnp.exp(steps * math.log(-root_value))
    return jnp.where(even, size, -size)


far_scale = inverse_gain * (
    first_coeff * (1.0 / root_value - root_value)
    + second_coeff * (root_value**-2 - root_value**2)
)
near_shift = inverse_gain * second_coeff * (root_value - 1.0 / root_value)


def stencil_block(length):
    source = lax.broadcasted_iota(jnp.int32, (length, length), 0)
    target = lax.broadcasted_iota(jnp.int32, (length, length), 1)
    offset = source - target
    steps = jnp.abs(offset).astype(jnp.float32)
    size = far_scale * root_power(steps) + jnp.where(steps == 1.0, near_shift, 0.0)
    return jnp.where(offset > 0, size, jnp.where(offset < 0, -size, 0.0))


def edge_weights(length):
    row = lax.broadcasted_iota(jnp.int32, (8, length), 0)
    cell = lax.broadcasted_iota(jnp.int32, (8, length), 1)
    back = length - 1 - cell
    decay = root_power(jnp.where(row == 0, back, cell).astype(jnp.float32))
    edge = jnp.where(jnp.where(row == 1, back, cell) == 0, 1.0, 0.0)
    weights = jnp.where((row == 0) | (row == 2), decay, edge)
    return jnp.where(row < 4, weights, 0.0)


def edge_profiles(length):
    row = lax.broadcasted_iota(jnp.int32, (8, length), 0)
    cell = lax.broadcasted_iota(jnp.int32, (8, length), 1)
    back = length - 1 - cell
    depth = jnp.where(row < 2, cell, back)
    decay = far_scale * root_power((depth + 1).astype(jnp.float32))
    edge = jnp.where(depth == 0, near_shift, 0.0)
    profile = jnp.where((row == 0) | (row == 2), decay, edge)
    return jnp.where(row < 2, -profile, jnp.where(row < 4, profile, 0.0))


def stacked_high(values):
    high = values.astype(jnp.bfloat16).astype(jnp.float32)
    rest = values - high
    return jnp.concatenate([high, high, rest, rest], axis=0).astype(jnp.bfloat16)


def stacked_both(values):
    high = values.astype(jnp.bfloat16).astype(jnp.float32)
    rest = values - high
    return jnp.concatenate([high, rest, high, rest], axis=0).astype(jnp.bfloat16)


def down(left, right):
    return lax.dot_general(
        left, right, (((0,), (0,)), ((), ())), preferred_element_type=jnp.float32
    )


def edge_sums(edges, values):
    high, low = split(values)
    dims = (((1,), (1,)), ((), ()))
    sums = lax.dot_general(edges, high, dims, preferred_element_type=jnp.float32)
    rest = lax.dot_general(edges, low, dims, preferred_element_type=jnp.float32)
    return sums[:8] + sums[8:] + rest[:8]


def through_stencil(values, stencil):
    high, low = split(values)
    slope = jnp.dot(high, stencil[0], preferred_element_type=jnp.float32)
    slope = slope + jnp.dot(low, stencil[0], preferred_element_type=jnp.float32)
    return slope + jnp.dot(high, stencil[1], preferred_element_type=jnp.float32)


def exchange_kernel(
    n, streams, fields, planes, rows, length, share, depth, wide,
    cot_hbm, low_hbm, pivot_hbm, speed_hbm,
    base, carried_out, slope_out, columns,
    cot, low_ref, pivot_ref, speed_ref, sent, got, answer, carried,
    lines_left, lines_right, lines_from_left, lines_from_right, ends, ends_got,
    to_left, to_right, from_left, from_right, stencil,
    load_sem, row_sem, send1, recv1, send2, recv2, send3, recv3, send4, recv4, send5, recv5,
):
    wall = lax.axis_index("wall")
    stream = lax.axis_index("stream")
    right = lax.rem(stream + 1, streams)
    left = lax.rem(stream + streams - 1, streams)

    row_loads = [
        pltpu.make_async_copy(source, target, row_sem.at[i])
        for i, (source, target) in enumerate(
            ((low_hbm, low_ref), (pivot_hbm, pivot_ref), (speed_hbm, speed_ref))
        )
    ]
    for load in row_loads:
        load.start()
    loads = [
        pltpu.make_async_copy(cot_hbm.at[f], cot.at[f], load_sem.at[f]) for f in range(fields)
    ]
    for load in loads:
        load.start()

    barrier = pltpu.get_barrier_semaphore()
    for d in range(1, n):
        pl.semaphore_signal(
            barrier, inc=1, device_id={"wall": lax.rem(wall + d, n)}, device_id_type=MESH
        )
    for side in (left, right):
        pl.semaphore_signal(barrier, inc=1, device_id={"stream": side}, device_id_type=MESH)

    def swap(source, target, send, recv, d):
        peer = lax.rem(wall + d, n)
        return pltpu.make_async_remote_copy(
            src_ref=source.at[peer], dst_ref=target.at[wall],
            send_sem=send.at[peer], recv_sem=recv.at[wall],
            device_id={"wall": peer}, device_id_type=MESH,
        )

    def arrive(source, target, send, recv, d):
        peer = lax.rem(wall + d, n)
        pltpu.make_async_remote_copy(
            src_ref=source.at[peer], dst_ref=target.at[peer],
            send_sem=send.at[peer], recv_sem=recv.at[peer],
            device_id={"wall": peer}, device_id_type=MESH,
        ).wait_recv()

    def beside(pairs, send, recv):
        return [
            pltpu.make_async_remote_copy(
                src_ref=source, dst_ref=target, send_sem=send.at[i], recv_sem=recv.at[i],
                device_id={"stream": side}, device_id_type=MESH,
            )
            for i, (source, target, side) in enumerate(pairs)
        ]

    sent[...] = jnp.zeros(sent.shape, jnp.float32)
    weights = edge_weights(length)
    high = weights.astype(jnp.bfloat16).astype(jnp.float32)
    edges = jnp.concatenate([high, weights - high], axis=0).astype(jnp.bfloat16)

    for i, part in enumerate(split(stencil_block(length))):
        stencil[i] = part
    profiles = stacked_both(edge_profiles(length))

    lanes = 4 * rows
    total = fields * rows
    row_at = lax.rem(lax.broadcasted_iota(jnp.int32, (total, lanes), 0), rows)
    col_at = lax.rem(lax.broadcasted_iota(jnp.int32, (total, lanes), 1), rows)
    small_row = lax.broadcasted_iota(jnp.int32, (rows, rows), 0)
    small_col = lax.broadcasted_iota(jnp.int32, (rows, rows), 1)

    def column(ref, shift):
        pick = small_row == small_col + shift
        return jnp.concatenate(
            [
                jnp.sum(jnp.where(pick, ref[f : f + 1, :], 0.0), axis=1, keepdims=True)
                for f in range(fields)
            ],
            axis=0,
        )

    for load in row_loads:
        load.wait()
    before = column(low_ref, 1)
    inverse_pivot = 1.0 / column(pivot_ref, 0)
    speed = column(speed_ref, 0)
    product = jnp.where(row_at > col_at, before, 1.0)
    step = 1
    while step < rows:
        product = product * jnp.where(row_at >= step, pltpu.roll(product, step, 0), 1.0)
        step *= 2
    factor = jnp.where(row_at >= col_at, product, 0.0)
    weighted = factor * inverse_pivot

    lane = lax.broadcasted_iota(jnp.int32, (rows, lanes), 1)
    wide_row = lax.broadcasted_iota(jnp.int32, (rows, lanes), 0)
    coeff_lane = lax.broadcasted_iota(jnp.int32, (1, length), 1)
    line_lane = lax.broadcasted_iota(jnp.int32, (1, wide), 1)
    line_index = (line_lane // depth) * share + line_lane % depth
    line_used = (line_lane % depth < share) & (line_index < fields * planes)
    line_field = jnp.where(line_used, line_index // planes, -1)
    half = length // 2
    spreads, leaves, speeds = [], [], []
    coeffs = jnp.zeros((1, length), jnp.float32)
    line_through = jnp.zeros((1, wide), jnp.float32)
    line_first = jnp.zeros((1, wide), jnp.float32)
    for f in range(fields):
        span = slice(f * rows, (f + 1) * rows)
        last = low_ref[f : f + 1, rows - 1 : rows]
        leave_row = factor[(f + 1) * rows - 1 : (f + 1) * rows] * last
        spread_row = jnp.sum(weighted[span] * factor[span, 0:1], axis=0, keepdims=True)
        leave = jnp.sum(jnp.where(lane == wide_row, leave_row, 0.0), axis=1, keepdims=True)
        spread = jnp.sum(jnp.where(lane == wide_row, spread_row, 0.0), axis=1, keepdims=True)
        coeffs = coeffs + jnp.where(coeff_lane == f, leave_row[:, 0:1], 0.0)
        coeffs = coeffs + jnp.where(coeff_lane == half + f, spread_row[:, 0:1], 0.0)
        line_through = line_through + jnp.where(line_field == f, leave_row[:, 0:1], 0.0)
        line_first = line_first + jnp.where(line_field == f, spread_row[:, 0:1], 0.0)
        spreads.append(jnp.broadcast_to(spread, (rows, length)))
        leaves.append(jnp.broadcast_to(leave, (rows, length)))
        speeds.append(jnp.broadcast_to(speed[span], (rows, length)))
        columns[0, f] = spreads[f][:, :128]
        columns[1, f] = leaves[f][:, :128]
        columns[2, f] = spreads[f][:, :128] * speeds[f][:, :128]
        columns[3, f] = leaves[f][:, :128] * speeds[f][:, :128]
    for o in range(n):
        sent[o, 2 * share : 2 * share + 1, :] = coeffs

    for f in range(fields):
        loads[f].wait()
        for z in range(planes):
            line = f * planes + z
            values = cot[f, z]
            sent[line // share, line % share, :] = jnp.sum(values * leaves[f], axis=0)
            sent[line // share, share + line % share, :] = jnp.sum(values * spreads[f], axis=0)

    pl.semaphore_wait(barrier, n + 1)

    first = [swap(sent, got, send1, recv1, d) for d in range(1, n)]
    for copy in first:
        copy.start()
    got[wall] = sent[wall]

    flat = sent[...].reshape(n * depth, length)
    if wide > n * depth:
        flat = jnp.concatenate(
            [flat, jnp.zeros((wide - n * depth, length), jnp.float32)], axis=0
        )
    sums = edge_sums(edges, flat)
    lines_right[...] = sums[0:2]
    lines_left[...] = sums[2:4]
    lines_copies = beside(
        ((lines_right, lines_from_left, right), (lines_left, lines_from_right, left)), send3, recv3
    )
    for copy in lines_copies:
        copy.start()

    def settle_field(f):
        span = slice(f * rows, (f + 1) * rows)
        gram = lax.dot_general(
            weighted[span], factor[span], (((0,), (0,)), ((), ())),
            precision=lax.Precision.HIGHEST, preferred_element_type=jnp.float32,
        )[:rows]
        high = gram.astype(jnp.bfloat16).astype(jnp.float32)
        operator = jnp.where(lane < 2 * rows, high, gram - high).astype(jnp.bfloat16)
        for z in range(planes):
            high, low = split(cot[f, z])
            out = jnp.dot(
                operator,
                jnp.concatenate([high, low, high, low], axis=0),
                preferred_element_type=jnp.float32,
            )
            base[f, z] = out
            cot[f, z] = speeds[f] * out
        sums = edge_sums(edges, cot[f].reshape(planes * rows, length))
        to_right[f] = sums[0:2]
        to_left[f] = sums[2:4]

    for f in range(fields):
        settle_field(f)
    edge_copies = beside(
        ((to_right, from_left, right), (to_left, from_right, left)), send5, recv5
    )
    for copy in edge_copies:
        copy.start()

    for d in range(1, n):
        arrive(sent, got, send1, recv1, d)

    share_field = (wall * share + lax.broadcasted_iota(jnp.int32, (share, length), 0)) // planes
    share_lane = lax.broadcasted_iota(jnp.int32, (share, length), 1)
    incoming = jnp.zeros((share, length), jnp.float32)
    through, crest = [], []
    for b in range(n):
        coeff_row = got[b, 2 * share : 2 * share + 1, :]
        t = jnp.sum(jnp.where(share_lane == share_field, coeff_row, 0.0), axis=1, keepdims=True)
        p = jnp.sum(
            jnp.where(share_lane == share_field + half, coeff_row, 0.0), axis=1, keepdims=True
        )
        answer[b, 0:share, :] = incoming
        through.append(t)
        crest.append(got[b, share : 2 * share, :] + p * incoming)
        incoming = t * incoming + got[b, 0:share, :]
    descent = jnp.zeros((share, length), jnp.float32)
    for b in range(n - 1, -1, -1):
        answer[b, share : 2 * share, :] = descent
        answer[b, 2 * share :, :] = jnp.zeros((depth - 2 * share, length), jnp.float32)
        descent = through[b] * descent + crest[b]

    second = [swap(answer, carried, send2, recv2, d) for d in range(1, n)]
    for copy in second:
        copy.start()
    carried[wall] = answer[wall]

    for copy in lines_copies:
        copy.wait_recv()
    ends[0:2, :] = lines_from_left[...]
    ends[2:4, :] = lines_from_right[...]
    ends[4:5, :] = line_through
    ends[5:6, :] = line_first
    ends[6:8, :] = jnp.zeros((2, wide), jnp.float32)
    gather = [
        pltpu.make_async_remote_copy(
            src_ref=ends, dst_ref=ends_got.at[wall],
            send_sem=send4.at[lax.rem(wall + d, n)], recv_sem=recv4.at[wall],
            device_id={"wall": lax.rem(wall + d, n)}, device_id_type=MESH,
        )
        for d in range(1, n)
    ]
    for copy in gather:
        copy.start()
    ends_got[wall] = ends[...]

    blank = jnp.zeros((4, planes * rows), jnp.float32)
    ready = fields // 2
    for f in range(fields):
        if f == ready:
            for copy in edge_copies:
                copy.wait_recv()
        slope = through_stencil(cot[f].reshape(planes * rows, length), stencil)
        if f >= ready:
            sides = jnp.concatenate([from_left[f], from_right[f], blank], axis=0)
            slope = slope + down(stacked_high(sides), profiles)
        base[f] = base[f] + slope.reshape(planes, rows, length)
    for f in range(ready):
        sides = jnp.concatenate([from_left[f], from_right[f], blank], axis=0)
        slope = down(stacked_high(sides), profiles)
        base[f] = base[f] + slope.reshape(planes, rows, length)

    for d in range(1, n):
        peer = lax.rem(wall + d, n)
        pltpu.make_async_remote_copy(
            src_ref=ends, dst_ref=ends_got.at[peer],
            send_sem=send4.at[peer], recv_sem=recv4.at[peer],
            device_id={"wall": peer}, device_id_type=MESH,
        ).wait_recv()
    zero = jnp.zeros((8, wide), jnp.float32)
    incoming, taken_up, through, crest = zero, zero, [], []
    for b in range(n):
        arrived = ends_got[b]
        t, p = arrived[4:5], arrived[5:6]
        taken_up = jnp.where(wall == b, incoming, taken_up)
        through.append(t)
        crest.append(pltpu.roll(arrived, wide - share, 1) + p * incoming)
        incoming = t * incoming + arrived
    descent, taken_down = zero, zero
    for b in range(n - 1, -1, -1):
        taken_down = jnp.where(wall == b, descent, taken_down)
        descent = through[b] * descent + crest[b]
    side_rows = lax.broadcasted_iota(jnp.int32, (8, wide), 0) < 4
    used = side_rows & line_used
    taken_up = jnp.where(used, taken_up, 0.0)
    taken_down = jnp.where(used, taken_down, 0.0)
    halo = down(stacked_high(taken_up + pltpu.roll(taken_down, share, 1)), profiles)

    for d in range(1, n):
        arrive(answer, carried, send2, recv2, d)
    flat = carried[...].reshape(n * depth, length)
    slope = through_stencil(flat, stencil) + halo[: n * depth]
    carried_out[...] = carried[...]
    slope_out[...] = slope.reshape(n, depth, length)

    for copy in first + second + lines_copies + gather + edge_copies:
        copy.wait_send()


def gather_kernel(
    fields, planes, rows, length, share, base, carried, slopes, columns, out_hbm, out, store_sem
):
    stores = []
    piece = math.gcd(planes, 4)
    for f in range(fields):
        spread, leave, spread_speed, leave_speed = (
            jnp.concatenate([columns[i, f]] * (length // 128), axis=1) for i in range(4)
        )
        for z in range(planes):
            line = f * planes + z
            o, up = line // share, line % share
            low = share + up
            value = base[f, z] + spread * carried[o, up : up + 1, :]
            value = value + leave * carried[o, low : low + 1, :]
            value = value + spread_speed * slopes[o, up : up + 1, :]
            out[f, z] = value + leave_speed * slopes[o, low : low + 1, :]
            if z % piece == piece - 1:
                part = pl.ds(z + 1 - piece, piece)
                store = pltpu.make_async_copy(
                    out.at[f, part], out_hbm.at[f, part], store_sem.at[len(stores)]
                )
                store.start()
                stores.append(store)
    for store in stores:
        store.wait()


def local(n, streams, cotangent, lower, pivot, speed):
    fields, planes, rows, length = cotangent.shape
    share = -(-fields * planes // n)
    depth = up_to(2 * share + 1, 8)
    wide = up_to(n * depth, 128)
    edge_shape = (fields, 2, planes * rows)
    line_shape = (n, depth, length)
    column_shape = (4, fields, rows, 128)
    vmem = pl.BlockSpec(memory_space=pltpu.VMEM)
    hbm = pl.BlockSpec(memory_space=pltpu.HBM)
    f32 = jnp.float32
    dma = pltpu.SemaphoreType.DMA
    scratch = lambda shape: pltpu.VMEM(shape, f32)
    out_shapes = (cotangent.shape, line_shape, line_shape, column_shape)
    parts = pl.pallas_call(
        functools.partial(
            exchange_kernel, n, streams, fields, planes, rows, length, share, depth, wide
        ),
        out_shape=tuple(jax.ShapeDtypeStruct(shape, f32) for shape in out_shapes),
        in_specs=[hbm] * 4,
        out_specs=(vmem,) * 4,
        scratch_shapes=[scratch(cotangent.shape)]
        + [scratch(lower.shape)] * 3
        + [scratch(line_shape)] * 4
        + [scratch((2, wide))] * 4
        + [scratch((8, wide)), scratch((n, 8, wide))]
        + [scratch(edge_shape)] * 4
        + [pltpu.VMEM((2, length, length), jnp.bfloat16)]
        + [dma((fields,)), dma((3,))]
        + [dma((n,))] * 4
        + [dma((2,))] * 2
        + [dma((n,))] * 2
        + [dma((2,))] * 2,
        compiler_params=pltpu.CompilerParams(
            collective_id=0, has_side_effects=True, vmem_limit_bytes=VMEM_LIMIT
        ),
    )(*[
        pltpu.with_memory_space_constraint(a, pltpu.HBM)
        for a in (cotangent, lower, pivot, speed)
    ])
    return pl.pallas_call(
        functools.partial(gather_kernel, fields, planes, rows, length, share),
        out_shape=jax.ShapeDtypeStruct(cotangent.shape, f32),
        in_specs=[vmem] * 4,
        out_specs=hbm,
        scratch_shapes=[scratch(cotangent.shape), dma((fields * planes,))],
        compiler_params=pltpu.CompilerParams(vmem_limit_bytes=VMEM_LIMIT),
    )(*parts)


def solution(mesh):
    return jax.shard_map(
        functools.partial(local, mesh.shape["wall"], mesh.shape["stream"]),
        mesh=mesh,
        in_specs=(
            P(None, None, "wall", "stream"),
            P(None, "wall"),
            P(None, "wall"),
            P(None, "wall"),
        ),
        out_specs=P(None, None, "wall", "stream"),
        check_vma=False,
    )
```

```python
import functools
import math

import jax
import jax.numpy as jnp
from jax import lax
from jax.experimental import pallas as pl
from jax.experimental.pallas import tpu as pltpu
from jax.sharding import PartitionSpec as P

root_value = (math.sqrt(5.0) - 3.0) / 2.0
inverse_gain = 3.0 / math.sqrt(5.0)
first_coeff = 7.0 / 9.0
second_coeff = 1.0 / 36.0
MESH = pl.DeviceIdType.MESH
VMEM_LIMIT = 40 * 1024 * 1024


def up_to(value, unit):
    return -(-value // unit) * unit


def split(values):
    high = values.astype(jnp.bfloat16)
    low = (values - high.astype(jnp.float32)).astype(jnp.bfloat16)
    return high, low


def root_power(steps):
    even = steps - 2.0 * jnp.floor(steps * 0.5) == 0.0
    size = jnp.exp(steps * math.log(-root_value))
    return jnp.where(even, size, -size)


far_scale = inverse_gain * (
    first_coeff * (1.0 / root_value - root_value)
    + second_coeff * (root_value**-2 - root_value**2)
)
near_shift = inverse_gain * second_coeff * (root_value - 1.0 / root_value)


def stencil_block(length):
    source = lax.broadcasted_iota(jnp.int32, (length, length), 0)
    target = lax.broadcasted_iota(jnp.int32, (length, length), 1)
    offset = source - target
    steps = jnp.abs(offset).astype(jnp.float32)
    size = far_scale * root_power(steps) + jnp.where(steps == 1.0, near_shift, 0.0)
    return jnp.where(offset > 0, size, jnp.where(offset < 0, -size, 0.0))


def edge_weights(length):
    cell = lax.broadcasted_iota(jnp.int32, (length, 128), 0)
    odd = lax.broadcasted_iota(jnp.int32, (length, 128), 1) % 2 == 1
    sides = []
    for depth in (length - 1 - cell, cell):
        edge = jnp.where(depth == 0, 1.0, 0.0)
        sides.append(jnp.where(odd, edge, root_power(depth.astype(jnp.float32))))
    return jnp.concatenate(sides, axis=1)


def edge_profiles(length):
    row = lax.broadcasted_iota(jnp.int32, (8, length), 0)
    cell = lax.broadcasted_iota(jnp.int32, (8, length), 1)
    back = length - 1 - cell
    depth = jnp.where(row < 2, cell, back)
    decay = far_scale * root_power((depth + 1).astype(jnp.float32))
    edge = jnp.where(depth == 0, near_shift, 0.0)
    profile = jnp.where((row == 0) | (row == 2), decay, edge)
    return jnp.where(row < 2, -profile, jnp.where(row < 4, profile, 0.0))


def stacked_both(values):
    high, low = split(values)
    return jnp.concatenate([high, low, high, low], axis=0)


def through_stencil(values, stencil):
    high, low = split(values)
    slope = jnp.dot(high, stencil[0], preferred_element_type=jnp.float32)
    slope = slope + jnp.dot(low, stencil[0], preferred_element_type=jnp.float32)
    return slope + jnp.dot(high, stencil[1], preferred_element_type=jnp.float32)


def exchange_kernel(
    n, streams, fields, planes, rows, length, share, depth, pack,
    cot_hbm, low_hbm, pivot_hbm, speed_hbm,
    base, carried_out, slope_out, columns,
    cot, low_ref, pivot_ref, speed_ref, sent, got, answer, carried,
    ends, ends_got, line_sums, to_left, to_right, from_left, from_right, stencil, weights, profiles,
    load_sem, row_sem, send1, recv1, send2, recv2, send3, recv3, send4, recv4,
):
    wall = lax.axis_index("wall")
    stream = lax.axis_index("stream")
    right = lax.rem(stream + 1, streams)
    left = lax.rem(stream + streams - 1, streams)

    row_loads = [
        pltpu.make_async_copy(source, target, row_sem.at[i])
        for i, (source, target) in enumerate(
            ((low_hbm, low_ref), (pivot_hbm, pivot_ref), (speed_hbm, speed_ref))
        )
    ]
    for load in row_loads:
        load.start()
    loads = [
        pltpu.make_async_copy(cot_hbm.at[f], cot.at[f], load_sem.at[f]) for f in range(fields)
    ]
    for load in loads:
        load.start()

    barrier = pltpu.get_barrier_semaphore()
    for d in range(1, n):
        pl.semaphore_signal(
            barrier, inc=1, device_id={"wall": lax.rem(wall + d, n)}, device_id_type=MESH
        )
    for side in (left, right):
        pl.semaphore_signal(barrier, inc=1, device_id={"stream": side}, device_id_type=MESH)

    def swap(source, target, send, recv, d):
        peer = lax.rem(wall + d, n)
        return pltpu.make_async_remote_copy(
            src_ref=source.at[peer], dst_ref=target.at[wall],
            send_sem=send.at[peer], recv_sem=recv.at[wall],
            device_id={"wall": peer}, device_id_type=MESH,
        )

    def arrive(source, target, send, recv, d):
        peer = lax.rem(wall + d, n)
        pltpu.make_async_remote_copy(
            src_ref=source.at[peer], dst_ref=target.at[peer],
            send_sem=send.at[peer], recv_sem=recv.at[peer],
            device_id={"wall": peer}, device_id_type=MESH,
        ).wait_recv()

    def beside(pairs, send, recv):
        return [
            pltpu.make_async_remote_copy(
                src_ref=source, dst_ref=target, send_sem=send.at[i], recv_sem=recv.at[i],
                device_id={"stream": side}, device_id_type=MESH,
            )
            for i, (source, target, side) in enumerate(pairs)
        ]

    sent[...] = jnp.zeros(sent.shape, jnp.float32)
    for i, part in enumerate(split(edge_weights(length))):
        weights[i] = part
    for i, part in enumerate(split(stencil_block(length))):
        stencil[i] = part

    lanes = 4 * rows
    total = fields * rows
    row_at = lax.rem(lax.broadcasted_iota(jnp.int32, (total, lanes), 0), rows)
    col_at = lax.rem(lax.broadcasted_iota(jnp.int32, (total, lanes), 1), rows)
    small_row = lax.broadcasted_iota(jnp.int32, (rows, rows), 0)
    small_col = lax.broadcasted_iota(jnp.int32, (rows, rows), 1)

    def column(ref, shift):
        pick = small_row == small_col + shift
        return jnp.concatenate(
            [
                jnp.sum(jnp.where(pick, ref[f : f + 1, :], 0.0), axis=1, keepdims=True)
                for f in range(fields)
            ],
            axis=0,
        )

    for load in row_loads:
        load.wait()
    before = column(low_ref, 1)
    inverse_pivot = 1.0 / column(pivot_ref, 0)
    speed = column(speed_ref, 0)
    product = jnp.where(row_at > col_at, before, 1.0)
    step = 1
    while step < rows:
        product = product * jnp.where(row_at >= step, pltpu.roll(product, step, 0), 1.0)
        step *= 2
    factor = jnp.where(row_at >= col_at, product, 0.0)
    weighted = factor * inverse_pivot

    lane = lax.broadcasted_iota(jnp.int32, (rows, lanes), 1)
    wide_row = lax.broadcasted_iota(jnp.int32, (rows, lanes), 0)
    coeff_lane = lax.broadcasted_iota(jnp.int32, (1, length), 1)
    groups = -(-fields // pack)
    place = lax.broadcasted_iota(jnp.int32, (1, 256), 1) % 128
    place_field = place // (2 * planes)
    half = length // 2
    spreads, leaves, speeds = [], [], []
    coeffs = jnp.zeros((1, length), jnp.float32)
    line_through = [jnp.zeros((1, 256), jnp.float32)] * groups
    line_first = [jnp.zeros((1, 256), jnp.float32)] * groups
    for f in range(fields):
        span = slice(f * rows, (f + 1) * rows)
        last = low_ref[f : f + 1, rows - 1 : rows]
        leave_row = factor[(f + 1) * rows - 1 : (f + 1) * rows] * last
        spread_row = jnp.sum(weighted[span] * factor[span, 0:1], axis=0, keepdims=True)
        leave = jnp.sum(jnp.where(lane == wide_row, leave_row, 0.0), axis=1, keepdims=True)
        spread = jnp.sum(jnp.where(lane == wide_row, spread_row, 0.0), axis=1, keepdims=True)
        coeffs = coeffs + jnp.where(coeff_lane == f, leave_row[:, 0:1], 0.0)
        coeffs = coeffs + jnp.where(coeff_lane == half + f, spread_row[:, 0:1], 0.0)
        here = place_field == f % pack
        line_through[f // pack] = jnp.where(here, leave_row[:, 0:1], line_through[f // pack])
        line_first[f // pack] = jnp.where(here, spread_row[:, 0:1], line_first[f // pack])
        spreads.append(jnp.broadcast_to(spread, (rows, length)))
        leaves.append(jnp.broadcast_to(leave, (rows, length)))
        speeds.append(jnp.broadcast_to(speed[span], (rows, length)))
        columns[0, f] = spreads[f][:, :128]
        columns[1, f] = leaves[f][:, :128]
        columns[2, f] = spreads[f][:, :128] * speeds[f][:, :128]
        columns[3, f] = leaves[f][:, :128] * speeds[f][:, :128]
    for o in range(n):
        sent[o, 2 * share : 2 * share + 1, :] = coeffs

    for f in range(fields):
        loads[f].wait()
        for z in range(planes):
            line = f * planes + z
            values = cot[f, z]
            sent[line // share, line % share, :] = jnp.sum(values * leaves[f], axis=0)
            sent[line // share, share + line % share, :] = jnp.sum(values * spreads[f], axis=0)

    pl.semaphore_wait(barrier, n + 1)

    first = [swap(sent, got, send1, recv1, d) for d in range(1, n)]
    for copy in first:
        copy.start()
    got[wall] = sent[wall]

    wide_place = lax.broadcasted_iota(jnp.int32, (rows, 256), 1) % 128 // 2
    for g in range(groups):
        tile = jnp.zeros((rows, 256), jnp.float32)
        for f in range(g * pack, min(fields, (g + 1) * pack)):
            sums = through_stencil(cot[f].reshape(planes * rows, length), weights)
            for z in range(planes):
                mine = wide_place == planes * (f % pack) + z
                tile = jnp.where(mine, sums[z * rows : (z + 1) * rows], tile)
        to_right[g] = tile[:, :128]
        to_left[g] = tile[:, 128:]
    edge_copies = beside(
        ((to_right, from_left, right), (to_left, from_right, left)), send3, recv3
    )
    for copy in edge_copies:
        copy.start()

    profile = edge_profiles(length)
    lane_at = lax.broadcasted_iota(jnp.int32, (128, length), 0)
    profile = jnp.concatenate(
        [
            jnp.where(lane_at % 2 == 0, profile[i : i + 1], profile[i + 1 : i + 2])
            for i in (0, 2)
        ],
        axis=0,
    )
    high = profile.astype(jnp.bfloat16).astype(jnp.float32)
    rest = profile - high
    slot = lax.broadcasted_iota(jnp.int32, (256, length), 0) % 128 // (2 * planes)
    mixed = jnp.where(slot < 2, high, jnp.where(slot == 2, rest, 0.0))
    profiles[0] = high.astype(jnp.bfloat16)
    profiles[1] = rest.astype(jnp.bfloat16)
    profiles[2] = mixed.astype(jnp.bfloat16)

    operators = []

    def settle_field(f):
        span = slice(f * rows, (f + 1) * rows)
        gram = lax.dot_general(
            weighted[span], factor[span], (((0,), (0,)), ((), ())),
            precision=lax.Precision.HIGHEST, preferred_element_type=jnp.float32,
        )[:rows]
        high = gram.astype(jnp.bfloat16).astype(jnp.float32)
        operator = jnp.where(lane < 2 * rows, high, gram - high).astype(jnp.bfloat16)
        operators.append(operator)
        for z in range(planes):
            high, low = split(cot[f, z])
            out = jnp.dot(
                operator,
                jnp.concatenate([high, low, high, low], axis=0),
                preferred_element_type=jnp.float32,
            )
            base[f, z] = out
            cot[f, z] = speeds[f] * out

    for f in range(fields):
        settle_field(f)
    for d in range(1, n):
        arrive(sent, got, send1, recv1, d)

    share_field = (wall * share + lax.broadcasted_iota(jnp.int32, (share, length), 0)) // planes
    share_lane = lax.broadcasted_iota(jnp.int32, (share, length), 1)
    incoming = jnp.zeros((share, length), jnp.float32)
    through, crest = [], []
    for b in range(n):
        coeff_row = got[b, 2 * share : 2 * share + 1, :]
        t = jnp.sum(jnp.where(share_lane == share_field, coeff_row, 0.0), axis=1, keepdims=True)
        p = jnp.sum(
            jnp.where(share_lane == share_field + half, coeff_row, 0.0), axis=1, keepdims=True
        )
        answer[b, 0:share, :] = incoming
        through.append(t)
        crest.append(got[b, share : 2 * share, :] + p * incoming)
        incoming = t * incoming + got[b, 0:share, :]
    descent = jnp.zeros((share, length), jnp.float32)
    for b in range(n - 1, -1, -1):
        answer[b, share : 2 * share, :] = descent
        answer[b, 2 * share :, :] = jnp.zeros((depth - 2 * share, length), jnp.float32)
        descent = through[b] * descent + crest[b]

    second = [swap(answer, carried, send2, recv2, d) for d in range(1, n)]
    for copy in second:
        copy.start()
    carried[wall] = answer[wall]

    for copy in edge_copies:
        copy.wait_recv()
    beyond = [jnp.concatenate([from_left[g], from_right[g]], axis=1) for g in range(groups)]
    for g in range(groups):
        lift = jnp.zeros((1, 256), jnp.float32)
        drop = lift
        for f in range(g * pack, min(fields, (g + 1) * pack)):
            here = place_field == f % pack
            leave, spread = leaves[f][:, :1], spreads[f][:, :1]
            lift = jnp.where(here, jnp.sum(leave * beyond[g], axis=0, keepdims=True), lift)
            drop = jnp.where(here, jnp.sum(spread * beyond[g], axis=0, keepdims=True), drop)
        ends[g : g + 1, :] = lift
        ends[groups + g : groups + g + 1, :] = drop
        ends[2 * groups + g : 2 * groups + g + 1, :] = line_through[g]
        ends[3 * groups + g : 3 * groups + g + 1, :] = line_first[g]
    if ends.shape[0] > 4 * groups:
        ends[4 * groups :, :] = jnp.zeros((ends.shape[0] - 4 * groups, 256), jnp.float32)
    gather = [
        pltpu.make_async_remote_copy(
            src_ref=ends, dst_ref=ends_got.at[wall],
            send_sem=send4.at[lax.rem(wall + d, n)], recv_sem=recv4.at[wall],
            device_id={"wall": lax.rem(wall + d, n)}, device_id_type=MESH,
        )
        for d in range(1, n)
    ]
    for copy in gather:
        copy.start()
    ends_got[wall] = ends[...]

    width = 2 * planes
    narrow = lax.broadcasted_iota(jnp.int32, (rows, 128), 1)
    wide_plane = lax.broadcasted_iota(jnp.int32, (rows, 256), 1) % width // 2
    for f in range(fields):
        slope = through_stencil(cot[f].reshape(planes * rows, length), stencil)
        sums = jnp.dot(
            operators[f], stacked_both(beyond[f // pack]), preferred_element_type=jnp.float32
        )
        sides = []
        for i in range(2):
            part = speeds[f][:, :128] * sums[:, 128 * i : 128 * (i + 1)]
            if f % pack:
                part = pltpu.roll(part, 128 - width * (f % pack), 1)
            part = jnp.where(narrow < width, part, 0.0)
            high = part.astype(jnp.bfloat16).astype(jnp.float32)
            sides.append(
                high + pltpu.roll(part - high, width, 1) + pltpu.roll(high, 2 * width, 1)
            )
        side = jnp.concatenate(sides, axis=1)
        spaced = jnp.concatenate(
            [jnp.where(wide_plane == z, side, 0.0) for z in range(planes)], axis=0
        )
        slope = slope + jnp.dot(
            spaced.astype(jnp.bfloat16), profiles[2], preferred_element_type=jnp.float32
        )
        base[f] = base[f] + slope.reshape(planes, rows, length)

    for d in range(1, n):
        peer = lax.rem(wall + d, n)
        pltpu.make_async_remote_copy(
            src_ref=ends, dst_ref=ends_got.at[peer],
            send_sem=send4.at[peer], recv_sem=recv4.at[peer],
            device_id={"wall": peer}, device_id_type=MESH,
        ).wait_recv()
    zero = jnp.zeros((groups, 256), jnp.float32)
    incoming, taken_up, through, crest = zero, zero, [], []
    for b in range(n):
        lift, drop, t, p = (ends_got[b, i * groups : (i + 1) * groups, :] for i in range(4))
        taken_up = jnp.where(wall == b, incoming, taken_up)
        through.append(t)
        crest.append(drop + p * incoming)
        incoming = t * incoming + lift
    descent, taken_down = zero, zero
    for b in range(n - 1, -1, -1):
        taken_down = jnp.where(wall == b, descent, taken_down)
        descent = through[b] * descent + crest[b]
    line_sums[...] = jnp.zeros(line_sums.shape, jnp.float32)
    for line in range(fields * planes):
        f, z = line // planes, line % planes
        g, o, up = f // pack, line // share, line % share
        mine = place // 2 == planes * (f % pack) + z
        line_sums[o, up : up + 1, :] = jnp.where(mine, taken_up[g : g + 1], 0.0)
        line_sums[o, share + up : share + up + 1, :] = jnp.where(mine, taken_down[g : g + 1], 0.0)
    halo = through_stencil(line_sums[...].reshape(n * depth, 256), profiles)

    for d in range(1, n):
        arrive(answer, carried, send2, recv2, d)
    flat = carried[...].reshape(n * depth, length)
    slope = through_stencil(flat, stencil) + halo
    carried_out[...] = carried[...]
    slope_out[...] = slope.reshape(n, depth, length)

    for copy in first + second + gather + edge_copies:
        copy.wait_send()


def gather_kernel(
    fields, planes, rows, length, share, base, carried, slopes, columns, out_hbm, out, store_sem
):
    stores = []
    for f in range(fields):
        spread, leave, spread_speed, leave_speed = (
            jnp.concatenate([columns[i, f]] * (length // 128), axis=1) for i in range(4)
        )
        for z in range(planes):
            line = f * planes + z
            o, up = line // share, line % share
            low = share + up
            value = base[f, z] + spread * carried[o, up : up + 1, :]
            value = value + leave * carried[o, low : low + 1, :]
            value = value + spread_speed * slopes[o, up : up + 1, :]
            out[f, z] = value + leave_speed * slopes[o, low : low + 1, :]
        store = pltpu.make_async_copy(out.at[f], out_hbm.at[f], store_sem.at[f])
        store.start()
        stores.append(store)
    for store in stores:
        store.wait()


def local(n, streams, cotangent, lower, pivot, speed):
    fields, planes, rows, length = cotangent.shape
    share = -(-fields * planes // n)
    depth = up_to(2 * share + 1, 8)
    pack = 128 // (2 * planes)
    groups = -(-fields // pack)
    end_rows = up_to(4 * groups, 8)
    edge_shape = (groups, rows, 128)
    line_shape = (n, depth, length)
    column_shape = (4, fields, rows, 128)
    vmem = pl.BlockSpec(memory_space=pltpu.VMEM)
    hbm = pl.BlockSpec(memory_space=pltpu.HBM)
    f32 = jnp.float32
    dma = pltpu.SemaphoreType.DMA
    scratch = lambda shape: pltpu.VMEM(shape, f32)
    out_shapes = (cotangent.shape, line_shape, line_shape, column_shape)
    parts = pl.pallas_call(
        functools.partial(
            exchange_kernel, n, streams, fields, planes, rows, length, share, depth, pack
        ),
        out_shape=tuple(jax.ShapeDtypeStruct(shape, f32) for shape in out_shapes),
        in_specs=[hbm] * 4,
        out_specs=(vmem,) * 4,
        scratch_shapes=[scratch(cotangent.shape)]
        + [scratch(lower.shape)] * 3
        + [scratch(line_shape)] * 4
        + [scratch((end_rows, 256)), scratch((n, end_rows, 256)), scratch((n, depth, 256))]
        + [scratch(edge_shape)] * 4
        + [pltpu.VMEM((2, length, length), jnp.bfloat16)]
        + [pltpu.VMEM((2, length, 256), jnp.bfloat16)]
        + [pltpu.VMEM((3, 256, length), jnp.bfloat16)]
        + [dma((fields,)), dma((3,))]
        + [dma((n,))] * 4
        + [dma((2,))] * 2
        + [dma((n,))] * 2,
        compiler_params=pltpu.CompilerParams(
            collective_id=0, has_side_effects=True, vmem_limit_bytes=VMEM_LIMIT
        ),
    )(*[
        pltpu.with_memory_space_constraint(a, pltpu.HBM)
        for a in (cotangent, lower, pivot, speed)
    ])
    return pl.pallas_call(
        functools.partial(gather_kernel, fields, planes, rows, length, share),
        out_shape=jax.ShapeDtypeStruct(cotangent.shape, f32),
        in_specs=[vmem] * 4,
        out_specs=hbm,
        scratch_shapes=[scratch(cotangent.shape), dma((fields,))],
        compiler_params=pltpu.CompilerParams(vmem_limit_bytes=VMEM_LIMIT),
    )(*parts)


def solution(mesh):
    return jax.shard_map(
        functools.partial(local, mesh.shape["wall"], mesh.shape["stream"]),
        mesh=mesh,
        in_specs=(
            P(None, None, "wall", "stream"),
            P(None, "wall"),
            P(None, "wall"),
            P(None, "wall"),
        ),
        out_specs=P(None, None, "wall", "stream"),
        check_vma=False,
    )
```

```python
import functools
import math

import jax
import jax.numpy as jnp
from jax import lax
from jax.experimental import pallas as pl
from jax.experimental.pallas import tpu as pltpu
from jax.sharding import PartitionSpec as P

root_value = (math.sqrt(5.0) - 3.0) / 2.0
inverse_gain = 3.0 / math.sqrt(5.0)
first_coeff = 7.0 / 9.0
second_coeff = 1.0 / 36.0
MESH = pl.DeviceIdType.MESH
VMEM_LIMIT = 40 * 1024 * 1024


def up_to(value, unit):
    return -(-value // unit) * unit


def split(values):
    high = values.astype(jnp.bfloat16)
    low = (values - high.astype(jnp.float32)).astype(jnp.bfloat16)
    return high, low


def root_power(steps):
    even = steps - 2.0 * jnp.floor(steps * 0.5) == 0.0
    size = jnp.exp(steps * math.log(-root_value))
    return jnp.where(even, size, -size)


far_scale = inverse_gain * (
    first_coeff * (1.0 / root_value - root_value)
    + second_coeff * (root_value**-2 - root_value**2)
)
near_shift = inverse_gain * second_coeff * (root_value - 1.0 / root_value)


def stencil_block(length):
    source = lax.broadcasted_iota(jnp.int32, (length, length), 0)
    target = lax.broadcasted_iota(jnp.int32, (length, length), 1)
    offset = source - target
    steps = jnp.abs(offset).astype(jnp.float32)
    size = far_scale * root_power(steps) + jnp.where(steps == 1.0, near_shift, 0.0)
    return jnp.where(offset > 0, size, jnp.where(offset < 0, -size, 0.0))


def edge_weights(length):
    cell = lax.broadcasted_iota(jnp.int32, (length, 128), 0)
    odd = lax.broadcasted_iota(jnp.int32, (length, 128), 1) % 2 == 1
    sides = []
    for depth in (length - 1 - cell, cell):
        edge = jnp.where(depth == 0, 1.0, 0.0)
        sides.append(jnp.where(odd, edge, root_power(depth.astype(jnp.float32))))
    return jnp.concatenate(sides, axis=1)


def edge_profiles(length):
    row = lax.broadcasted_iota(jnp.int32, (8, length), 0)
    cell = lax.broadcasted_iota(jnp.int32, (8, length), 1)
    back = length - 1 - cell
    depth = jnp.where(row < 2, cell, back)
    decay = far_scale * root_power((depth + 1).astype(jnp.float32))
    edge = jnp.where(depth == 0, near_shift, 0.0)
    profile = jnp.where((row == 0) | (row == 2), decay, edge)
    return jnp.where(row < 2, -profile, jnp.where(row < 4, profile, 0.0))


def stacked_both(values):
    high, low = split(values)
    return jnp.concatenate([high, low, high, low], axis=0)


def through_stencil(values, stencil):
    high, low = split(values)
    slope = jnp.dot(high, stencil[0], preferred_element_type=jnp.float32)
    slope = slope + jnp.dot(low, stencil[0], preferred_element_type=jnp.float32)
    return slope + jnp.dot(high, stencil[1], preferred_element_type=jnp.float32)


def exchange_kernel(
    n, streams, fields, planes, rows, length, share, depth, pack,
    cot_hbm, low_hbm, pivot_hbm, speed_hbm,
    base, carried_out, slope_out, columns,
    cot, settle, row_values, low_ref, pivot_ref, speed_ref, sent, got, answer, carried,
    ends, ends_got, line_sums, to_left, to_right, from_left, from_right, stencil, weights, profiles,
    load_sem, row_sem, send1, recv1, send2, recv2, send3, recv3, send4, recv4,
):
    wall = lax.axis_index("wall")
    stream = lax.axis_index("stream")
    right = lax.rem(stream + 1, streams)
    left = lax.rem(stream + streams - 1, streams)

    row_loads = [
        pltpu.make_async_copy(source, target, row_sem.at[i])
        for i, (source, target) in enumerate(
            ((low_hbm, low_ref), (pivot_hbm, pivot_ref), (speed_hbm, speed_ref))
        )
    ]
    for load in row_loads:
        load.start()
    loads = [
        [
            pltpu.make_async_copy(
                cot_hbm.at[f, :, pl.ds(128 * h, 128)], cot.at[f, h], load_sem.at[f, h]
            )
            for h in range(length // 128)
        ]
        for f in range(fields)
    ]
    for load in loads:
        for part in load:
            part.start()

    barrier = pltpu.get_barrier_semaphore()
    for d in range(1, n):
        pl.semaphore_signal(
            barrier, inc=1, device_id={"wall": lax.rem(wall + d, n)}, device_id_type=MESH
        )
    for side in (left, right):
        pl.semaphore_signal(barrier, inc=1, device_id={"stream": side}, device_id_type=MESH)

    def swap(source, target, send, recv, d):
        peer = lax.rem(wall + d, n)
        return pltpu.make_async_remote_copy(
            src_ref=source.at[peer], dst_ref=target.at[wall],
            send_sem=send.at[peer], recv_sem=recv.at[wall],
            device_id={"wall": peer}, device_id_type=MESH,
        )

    def arrive(source, target, send, recv, d):
        peer = lax.rem(wall + d, n)
        pltpu.make_async_remote_copy(
            src_ref=source.at[peer], dst_ref=target.at[peer],
            send_sem=send.at[peer], recv_sem=recv.at[peer],
            device_id={"wall": peer}, device_id_type=MESH,
        ).wait_recv()

    def beside(pairs, send, recv):
        return [
            pltpu.make_async_remote_copy(
                src_ref=source, dst_ref=target, send_sem=send.at[i], recv_sem=recv.at[i],
                device_id={"stream": side}, device_id_type=MESH,
            )
            for i, (source, target, side) in enumerate(pairs)
        ]

    sent[...] = jnp.zeros(sent.shape, jnp.float32)
    for i, part in enumerate(split(edge_weights(length))):
        weights[i] = part
    for i, part in enumerate(split(stencil_block(length))):
        stencil[i] = part

    lanes = 4 * rows
    total = fields * rows
    row_at = lax.rem(lax.broadcasted_iota(jnp.int32, (total, lanes), 0), rows)
    col_at = lax.rem(lax.broadcasted_iota(jnp.int32, (total, lanes), 1), rows)
    small_row = lax.broadcasted_iota(jnp.int32, (rows, rows), 0)
    small_col = lax.broadcasted_iota(jnp.int32, (rows, rows), 1)

    def column(ref, shift):
        pick = small_row == small_col + shift
        return jnp.concatenate(
            [
                jnp.sum(jnp.where(pick, ref[f : f + 1, :], 0.0), axis=1, keepdims=True)
                for f in range(fields)
            ],
            axis=0,
        )

    for load in row_loads:
        load.wait()
    before = column(low_ref, 1)
    inverse_pivot = 1.0 / column(pivot_ref, 0)
    speed = column(speed_ref, 0)
    product = jnp.where(row_at > col_at, before, 1.0)
    step = 1
    while step < rows:
        product = product * jnp.where(row_at >= step, pltpu.roll(product, step, 0), 1.0)
        step *= 2
    factor = jnp.where(row_at >= col_at, product, 0.0)
    weighted = factor * inverse_pivot

    lane = lax.broadcasted_iota(jnp.int32, (rows, lanes), 1)
    wide_row = lax.broadcasted_iota(jnp.int32, (rows, lanes), 0)
    coeff_lane = lax.broadcasted_iota(jnp.int32, (1, length), 1)
    groups = -(-fields // pack)
    place = lax.broadcasted_iota(jnp.int32, (1, 256), 1) % 128
    place_field = place // (2 * planes)
    half = length // 2
    spreads, leaves, speeds = [], [], []
    coeffs = jnp.zeros((1, length), jnp.float32)
    line_through = [jnp.zeros((1, 256), jnp.float32)] * groups
    line_first = [jnp.zeros((1, 256), jnp.float32)] * groups
    for f in range(fields):
        span = slice(f * rows, (f + 1) * rows)
        last = low_ref[f : f + 1, rows - 1 : rows]
        leave_row = factor[(f + 1) * rows - 1 : (f + 1) * rows] * last
        spread_row = jnp.sum(weighted[span] * factor[span, 0:1], axis=0, keepdims=True)
        leave = jnp.sum(jnp.where(lane == wide_row, leave_row, 0.0), axis=1, keepdims=True)
        spread = jnp.sum(jnp.where(lane == wide_row, spread_row, 0.0), axis=1, keepdims=True)
        coeffs = coeffs + jnp.where(coeff_lane == f, leave_row[:, 0:1], 0.0)
        coeffs = coeffs + jnp.where(coeff_lane == half + f, spread_row[:, 0:1], 0.0)
        here = place_field == f % pack
        line_through[f // pack] = jnp.where(here, leave_row[:, 0:1], line_through[f // pack])
        line_first[f // pack] = jnp.where(here, spread_row[:, 0:1], line_first[f // pack])
        spreads.append(jnp.broadcast_to(spread, (rows, length)))
        leaves.append(jnp.broadcast_to(leave, (rows, length)))
        speeds.append(jnp.broadcast_to(speed[span], (rows, length)))
        columns[0, f] = spreads[f][:, :128]
        columns[1, f] = leaves[f][:, :128]
        columns[2, f] = spreads[f][:, :128] * speeds[f][:, :128]
        columns[3, f] = leaves[f][:, :128] * speeds[f][:, :128]
    for o in range(n):
        sent[o, 2 * share : 2 * share + 1, :] = coeffs

    row_values[0] = jnp.broadcast_to(column(low_ref, 0), (total, 128))
    row_values[1] = jnp.broadcast_to(inverse_pivot, (total, 128))
    for f in range(fields):
        for load in loads[f]:
            load.wait()
        for h in range(length // 128):
            at = lambda j: (f, h, pl.ds(j, planes, stride=rows), slice(None))
            value = lambda i, j: row_values[i, f * rows + j : f * rows + j + 1, :]
            rising = cot[at(0)]
            scaled = [rising * value(1, 0)]
            for j in range(1, rows):
                rising = cot[at(j)] + value(0, j - 1) * rising
                scaled.append(rising * value(1, j))
            lift = value(0, rows - 1) * rising
            adjoint = scaled[rows - 1]
            settle[at(rows - 1)] = adjoint
            for j in range(rows - 2, -1, -1):
                adjoint = scaled[j] + value(0, j) * adjoint
                settle[at(j)] = adjoint
            lane_span = slice(128 * h, 128 * (h + 1))
            z = 0
            while z < planes:
                o, up = divmod(f * planes + z, share)
                run = min(planes - z, share - up)
                sent[o, up : up + run, lane_span] = lift[z : z + run]
                sent[o, share + up : share + up + run, lane_span] = adjoint[z : z + run]
                z += run

    pl.semaphore_wait(barrier, n + 1)

    first = [swap(sent, got, send1, recv1, d) for d in range(1, n)]
    for copy in first:
        copy.start()
    got[wall] = sent[wall]

    def joined(ref, f):
        return jnp.concatenate([ref[f, h] for h in range(length // 128)], axis=1)

    wide_place = lax.broadcasted_iota(jnp.int32, (rows, 256), 1) % 128 // 2
    for g in range(groups):
        tile = jnp.zeros((rows, 256), jnp.float32)
        for f in range(g * pack, min(fields, (g + 1) * pack)):
            sums = through_stencil(joined(cot, f), weights)
            for z in range(planes):
                mine = wide_place == planes * (f % pack) + z
                tile = jnp.where(mine, sums[z * rows : (z + 1) * rows], tile)
        to_right[g] = tile[:, :128]
        to_left[g] = tile[:, 128:]
    edge_copies = beside(
        ((to_right, from_left, right), (to_left, from_right, left)), send3, recv3
    )
    for copy in edge_copies:
        copy.start()

    profile = edge_profiles(length)
    lane_at = lax.broadcasted_iota(jnp.int32, (128, length), 0)
    profile = jnp.concatenate(
        [
            jnp.where(lane_at % 2 == 0, profile[i : i + 1], profile[i + 1 : i + 2])
            for i in (0, 2)
        ],
        axis=0,
    )
    high = profile.astype(jnp.bfloat16).astype(jnp.float32)
    rest = profile - high
    slot = lax.broadcasted_iota(jnp.int32, (256, length), 0) % 128 // (2 * planes)
    mixed = jnp.where(slot < 2, high, jnp.where(slot == 2, rest, 0.0))
    profiles[0] = high.astype(jnp.bfloat16)
    profiles[1] = rest.astype(jnp.bfloat16)
    profiles[2] = mixed.astype(jnp.bfloat16)

    operators = []

    def row_operator(f):
        span = slice(f * rows, (f + 1) * rows)
        gram = lax.dot_general(
            weighted[span], factor[span], (((0,), (0,)), ((), ())),
            precision=lax.Precision.HIGHEST, preferred_element_type=jnp.float32,
        )[:rows]
        high = gram.astype(jnp.bfloat16).astype(jnp.float32)
        operator = jnp.where(lane < 2 * rows, high, gram - high).astype(jnp.bfloat16)
        operators.append(operator)

    for f in range(fields):
        row_operator(f)
    for d in range(1, n):
        arrive(sent, got, send1, recv1, d)

    share_field = (wall * share + lax.broadcasted_iota(jnp.int32, (share, length), 0)) // planes
    share_lane = lax.broadcasted_iota(jnp.int32, (share, length), 1)
    incoming = jnp.zeros((share, length), jnp.float32)
    through, crest = [], []
    for b in range(n):
        coeff_row = got[b, 2 * share : 2 * share + 1, :]
        t = jnp.sum(jnp.where(share_lane == share_field, coeff_row, 0.0), axis=1, keepdims=True)
        p = jnp.sum(
            jnp.where(share_lane == share_field + half, coeff_row, 0.0), axis=1, keepdims=True
        )
        answer[b, 0:share, :] = incoming
        through.append(t)
        crest.append(got[b, share : 2 * share, :] + p * incoming)
        incoming = t * incoming + got[b, 0:share, :]
    descent = jnp.zeros((share, length), jnp.float32)
    for b in range(n - 1, -1, -1):
        answer[b, share : 2 * share, :] = descent
        answer[b, 2 * share :, :] = jnp.zeros((depth - 2 * share, length), jnp.float32)
        descent = through[b] * descent + crest[b]

    second = [swap(answer, carried, send2, recv2, d) for d in range(1, n)]
    for copy in second:
        copy.start()
    carried[wall] = answer[wall]

    for copy in edge_copies:
        copy.wait_recv()
    beyond = [jnp.concatenate([from_left[g], from_right[g]], axis=1) for g in range(groups)]
    for g in range(groups):
        lift = jnp.zeros((1, 256), jnp.float32)
        drop = lift
        for f in range(g * pack, min(fields, (g + 1) * pack)):
            here = place_field == f % pack
            leave, spread = leaves[f][:, :1], spreads[f][:, :1]
            lift = jnp.where(here, jnp.sum(leave * beyond[g], axis=0, keepdims=True), lift)
            drop = jnp.where(here, jnp.sum(spread * beyond[g], axis=0, keepdims=True), drop)
        ends[g : g + 1, :] = lift
        ends[groups + g : groups + g + 1, :] = drop
        ends[2 * groups + g : 2 * groups + g + 1, :] = line_through[g]
        ends[3 * groups + g : 3 * groups + g + 1, :] = line_first[g]
    if ends.shape[0] > 4 * groups:
        ends[4 * groups :, :] = jnp.zeros((ends.shape[0] - 4 * groups, 256), jnp.float32)
    gather = [
        pltpu.make_async_remote_copy(
            src_ref=ends, dst_ref=ends_got.at[wall],
            send_sem=send4.at[lax.rem(wall + d, n)], recv_sem=recv4.at[wall],
            device_id={"wall": lax.rem(wall + d, n)}, device_id_type=MESH,
        )
        for d in range(1, n)
    ]
    for copy in gather:
        copy.start()
    ends_got[wall] = ends[...]

    width = 2 * planes
    narrow = lax.broadcasted_iota(jnp.int32, (rows, 128), 1)
    wide_plane = lax.broadcasted_iota(jnp.int32, (rows, 256), 1) % width // 2
    for f in range(fields):
        solved = joined(settle, f)
        solved = solved.reshape(planes, rows, length)
        flux = (solved * speeds[f]).reshape(planes * rows, length)
        slope = through_stencil(flux, stencil)
        sums = jnp.dot(
            operators[f], stacked_both(beyond[f // pack]), preferred_element_type=jnp.float32
        )
        sides = []
        for i in range(2):
            part = speeds[f][:, :128] * sums[:, 128 * i : 128 * (i + 1)]
            if f % pack:
                part = pltpu.roll(part, 128 - width * (f % pack), 1)
            part = jnp.where(narrow < width, part, 0.0)
            high = part.astype(jnp.bfloat16).astype(jnp.float32)
            sides.append(
                high + pltpu.roll(part - high, width, 1) + pltpu.roll(high, 2 * width, 1)
            )
        side = jnp.concatenate(sides, axis=1)
        spaced = jnp.concatenate(
            [jnp.where(wide_plane == z, side, 0.0) for z in range(planes)], axis=0
        )
        slope = slope + jnp.dot(
            spaced.astype(jnp.bfloat16), profiles[2], preferred_element_type=jnp.float32
        )
        base[f] = solved + slope.reshape(planes, rows, length)

    for d in range(1, n):
        peer = lax.rem(wall + d, n)
        pltpu.make_async_remote_copy(
            src_ref=ends, dst_ref=ends_got.at[peer],
            send_sem=send4.at[peer], recv_sem=recv4.at[peer],
            device_id={"wall": peer}, device_id_type=MESH,
        ).wait_recv()
    zero = jnp.zeros((groups, 256), jnp.float32)
    incoming, taken_up, through, crest = zero, zero, [], []
    for b in range(n):
        lift, drop, t, p = (ends_got[b, i * groups : (i + 1) * groups, :] for i in range(4))
        taken_up = jnp.where(wall == b, incoming, taken_up)
        through.append(t)
        crest.append(drop + p * incoming)
        incoming = t * incoming + lift
    descent, taken_down = zero, zero
    for b in range(n - 1, -1, -1):
        taken_down = jnp.where(wall == b, descent, taken_down)
        descent = through[b] * descent + crest[b]
    line_sums[...] = jnp.zeros(line_sums.shape, jnp.float32)
    for line in range(fields * planes):
        f, z = line // planes, line % planes
        g, o, up = f // pack, line // share, line % share
        mine = place // 2 == planes * (f % pack) + z
        line_sums[o, up : up + 1, :] = jnp.where(mine, taken_up[g : g + 1], 0.0)
        line_sums[o, share + up : share + up + 1, :] = jnp.where(mine, taken_down[g : g + 1], 0.0)
    halo = through_stencil(line_sums[...].reshape(n * depth, 256), profiles)

    for d in range(1, n):
        arrive(answer, carried, send2, recv2, d)
    flat = carried[...].reshape(n * depth, length)
    slope = through_stencil(flat, stencil) + halo
    carried_out[...] = carried[...]
    slope_out[...] = slope.reshape(n, depth, length)

    for copy in first + second + gather + edge_copies:
        copy.wait_send()


def gather_kernel(
    fields, planes, rows, length, share, base, carried, slopes, columns, out_hbm, out, store_sem
):
    stores = []
    for f in range(fields):
        spread, leave, spread_speed, leave_speed = (
            jnp.concatenate([columns[i, f]] * (length // 128), axis=1) for i in range(4)
        )
        for z in range(planes):
            line = f * planes + z
            o, up = line // share, line % share
            low = share + up
            value = base[f, z] + spread * carried[o, up : up + 1, :]
            value = value + leave * carried[o, low : low + 1, :]
            value = value + spread_speed * slopes[o, up : up + 1, :]
            out[f, z] = value + leave_speed * slopes[o, low : low + 1, :]
        store = pltpu.make_async_copy(out.at[f], out_hbm.at[f], store_sem.at[f])
        store.start()
        stores.append(store)
    for store in stores:
        store.wait()


def local(n, streams, cotangent, lower, pivot, speed):
    fields, planes, rows, length = cotangent.shape
    share = -(-fields * planes // n)
    depth = up_to(2 * share + 1, 8)
    pack = 128 // (2 * planes)
    groups = -(-fields // pack)
    end_rows = up_to(4 * groups, 8)
    edge_shape = (groups, rows, 128)
    line_shape = (n, depth, length)
    column_shape = (4, fields, rows, 128)
    vmem = pl.BlockSpec(memory_space=pltpu.VMEM)
    hbm = pl.BlockSpec(memory_space=pltpu.HBM)
    f32 = jnp.float32
    dma = pltpu.SemaphoreType.DMA
    scratch = lambda shape: pltpu.VMEM(shape, f32)
    out_shapes = (cotangent.shape, line_shape, line_shape, column_shape)
    parts = pl.pallas_call(
        functools.partial(
            exchange_kernel, n, streams, fields, planes, rows, length, share, depth, pack
        ),
        out_shape=tuple(jax.ShapeDtypeStruct(shape, f32) for shape in out_shapes),
        in_specs=[hbm] * 4,
        out_specs=(vmem,) * 4,
        scratch_shapes=[scratch((fields, length // 128, planes * rows, 128))] * 2
        + [scratch((2, fields * rows, 128))]
        + [scratch(lower.shape)] * 3
        + [scratch(line_shape)] * 4
        + [scratch((end_rows, 256)), scratch((n, end_rows, 256)), scratch((n, depth, 256))]
        + [scratch(edge_shape)] * 4
        + [pltpu.VMEM((2, length, length), jnp.bfloat16)]
        + [pltpu.VMEM((2, length, 256), jnp.bfloat16)]
        + [pltpu.VMEM((3, 256, length), jnp.bfloat16)]
        + [dma((fields, length // 128)), dma((3,))]
        + [dma((n,))] * 4
        + [dma((2,))] * 2
        + [dma((n,))] * 2,
        compiler_params=pltpu.CompilerParams(
            collective_id=0, has_side_effects=True, vmem_limit_bytes=VMEM_LIMIT
        ),
    )(*[
        pltpu.with_memory_space_constraint(a, pltpu.HBM)
        for a in (cotangent.reshape(fields, planes * rows, length), lower, pivot, speed)
    ])
    return pl.pallas_call(
        functools.partial(gather_kernel, fields, planes, rows, length, share),
        out_shape=jax.ShapeDtypeStruct(cotangent.shape, f32),
        in_specs=[vmem] * 4,
        out_specs=hbm,
        scratch_shapes=[scratch(cotangent.shape), dma((fields,))],
        compiler_params=pltpu.CompilerParams(vmem_limit_bytes=VMEM_LIMIT),
    )(*parts)


def solution(mesh):
    return jax.shard_map(
        functools.partial(local, mesh.shape["wall"], mesh.shape["stream"]),
        mesh=mesh,
        in_specs=(
            P(None, None, "wall", "stream"),
            P(None, "wall"),
            P(None, "wall"),
            P(None, "wall"),
        ),
        out_specs=P(None, None, "wall", "stream"),
        check_vma=False,
    )
```

```python
import functools
import math

import jax
import jax.numpy as jnp
from jax import lax
from jax.experimental import pallas as pl
from jax.experimental.pallas import tpu as pltpu
from jax.sharding import PartitionSpec as P

root_value = (math.sqrt(5.0) - 3.0) / 2.0
inverse_gain = 3.0 / math.sqrt(5.0)
first_coeff = 7.0 / 9.0
second_coeff = 1.0 / 36.0
MESH = pl.DeviceIdType.MESH
VMEM_LIMIT = 40 * 1024 * 1024


def up_to(value, unit):
    return -(-value // unit) * unit


def split(values):
    high = values.astype(jnp.bfloat16)
    low = (values - high.astype(jnp.float32)).astype(jnp.bfloat16)
    return high, low


def root_power(steps):
    even = steps - 2.0 * jnp.floor(steps * 0.5) == 0.0
    size = jnp.exp(steps * math.log(-root_value))
    return jnp.where(even, size, -size)


far_scale = inverse_gain * (
    first_coeff * (1.0 / root_value - root_value)
    + second_coeff * (root_value**-2 - root_value**2)
)
near_shift = inverse_gain * second_coeff * (root_value - 1.0 / root_value)


def stencil_block(length):
    source = lax.broadcasted_iota(jnp.int32, (length, length), 0)
    target = lax.broadcasted_iota(jnp.int32, (length, length), 1)
    offset = source - target
    steps = jnp.abs(offset).astype(jnp.float32)
    size = far_scale * root_power(steps) + jnp.where(steps == 1.0, near_shift, 0.0)
    return jnp.where(offset > 0, size, jnp.where(offset < 0, -size, 0.0))


def edge_weights(length):
    cell = lax.broadcasted_iota(jnp.int32, (length, 128), 0)
    odd = lax.broadcasted_iota(jnp.int32, (length, 128), 1) % 2 == 1
    sides = []
    for depth in (length - 1 - cell, cell):
        edge = jnp.where(depth == 0, 1.0, 0.0)
        sides.append(jnp.where(odd, edge, root_power(depth.astype(jnp.float32))))
    return jnp.concatenate(sides, axis=1)


def edge_profiles(length):
    row = lax.broadcasted_iota(jnp.int32, (8, length), 0)
    cell = lax.broadcasted_iota(jnp.int32, (8, length), 1)
    back = length - 1 - cell
    depth = jnp.where(row < 2, cell, back)
    decay = far_scale * root_power((depth + 1).astype(jnp.float32))
    edge = jnp.where(depth == 0, near_shift, 0.0)
    profile = jnp.where((row == 0) | (row == 2), decay, edge)
    return jnp.where(row < 2, -profile, jnp.where(row < 4, profile, 0.0))


def stacked_both(values):
    high, low = split(values)
    return jnp.concatenate([high, low, high, low], axis=0)


def through_stencil(values, stencil):
    high, low = split(values)
    slope = jnp.dot(high, stencil[0], preferred_element_type=jnp.float32)
    slope = slope + jnp.dot(low, stencil[0], preferred_element_type=jnp.float32)
    return slope + jnp.dot(high, stencil[1], preferred_element_type=jnp.float32)


def exchange_kernel(
    n, streams, fields, planes, rows, length, share, depth, pack,
    cot_hbm, low_hbm, pivot_hbm, speed_hbm,
    base, carried_out, slope_out, columns,
    cot, settle, row_values, low_ref, pivot_ref, speed_ref, sent, got, answer, carried,
    ends, ends_got, line_sums, to_left, to_right, from_left, from_right, stencil, weights, profiles,
    load_sem, row_sem, send1, recv1, send2, recv2, send3, recv3, send4, recv4,
):
    wall = lax.axis_index("wall")
    stream = lax.axis_index("stream")
    right = lax.rem(stream + 1, streams)
    left = lax.rem(stream + streams - 1, streams)

    row_loads = [
        pltpu.make_async_copy(source, target, row_sem.at[i])
        for i, (source, target) in enumerate(
            ((low_hbm, low_ref), (pivot_hbm, pivot_ref), (speed_hbm, speed_ref))
        )
    ]
    for load in row_loads:
        load.start()
    loads = [
        [
            pltpu.make_async_copy(
                cot_hbm.at[f, :, pl.ds(128 * h, 128)], cot.at[f, h], load_sem.at[f, h]
            )
            for h in range(length // 128)
        ]
        for f in range(fields)
    ]
    for load in loads:
        for part in load:
            part.start()

    barrier = pltpu.get_barrier_semaphore()
    for d in range(1, n):
        pl.semaphore_signal(
            barrier, inc=1, device_id={"wall": lax.rem(wall + d, n)}, device_id_type=MESH
        )
    for side in (left, right):
        pl.semaphore_signal(barrier, inc=1, device_id={"stream": side}, device_id_type=MESH)

    def swap(source, target, send, recv, d):
        peer = lax.rem(wall + d, n)
        return pltpu.make_async_remote_copy(
            src_ref=source.at[peer], dst_ref=target.at[wall],
            send_sem=send.at[peer], recv_sem=recv.at[wall],
            device_id={"wall": peer}, device_id_type=MESH,
        )

    def arrive(source, target, send, recv, d):
        peer = lax.rem(wall + d, n)
        pltpu.make_async_remote_copy(
            src_ref=source.at[peer], dst_ref=target.at[peer],
            send_sem=send.at[peer], recv_sem=recv.at[peer],
            device_id={"wall": peer}, device_id_type=MESH,
        ).wait_recv()

    def beside(pairs, send, recv):
        return [
            pltpu.make_async_remote_copy(
                src_ref=source, dst_ref=target, send_sem=send.at[i], recv_sem=recv.at[i],
                device_id={"stream": side}, device_id_type=MESH,
            )
            for i, (source, target, side) in enumerate(pairs)
        ]

    sent[...] = jnp.zeros(sent.shape, jnp.float32)
    for i, part in enumerate(split(edge_weights(length))):
        weights[i] = part
    for i, part in enumerate(split(stencil_block(length))):
        stencil[i] = part

    lanes = 4 * rows
    total = fields * rows
    row_at = lax.rem(lax.broadcasted_iota(jnp.int32, (total, lanes), 0), rows)
    col_at = lax.rem(lax.broadcasted_iota(jnp.int32, (total, lanes), 1), rows)
    small_row = lax.broadcasted_iota(jnp.int32, (rows, rows), 0)
    small_col = lax.broadcasted_iota(jnp.int32, (rows, rows), 1)

    def column(ref, shift):
        pick = small_row == small_col + shift
        return jnp.concatenate(
            [
                jnp.sum(jnp.where(pick, ref[f : f + 1, :], 0.0), axis=1, keepdims=True)
                for f in range(fields)
            ],
            axis=0,
        )

    for load in row_loads:
        load.wait()
    before = column(low_ref, 1)
    inverse_pivot = 1.0 / column(pivot_ref, 0)
    speed = column(speed_ref, 0)
    product = jnp.where(row_at > col_at, before, 1.0)
    step = 1
    while step < rows:
        product = product * jnp.where(row_at >= step, pltpu.roll(product, step, 0), 1.0)
        step *= 2
    factor = jnp.where(row_at >= col_at, product, 0.0)
    weighted = factor * inverse_pivot

    lane = lax.broadcasted_iota(jnp.int32, (rows, lanes), 1)
    wide_row = lax.broadcasted_iota(jnp.int32, (rows, lanes), 0)
    coeff_lane = lax.broadcasted_iota(jnp.int32, (1, length), 1)
    groups = -(-fields // pack)
    place = lax.broadcasted_iota(jnp.int32, (1, 256), 1) % 128
    place_field = place // (2 * planes)
    half = length // 2
    spreads, leaves, speeds = [], [], []
    coeffs = jnp.zeros((1, length), jnp.float32)
    line_through = [jnp.zeros((1, 256), jnp.float32)] * groups
    line_first = [jnp.zeros((1, 256), jnp.float32)] * groups
    for f in range(fields):
        span = slice(f * rows, (f + 1) * rows)
        last = low_ref[f : f + 1, rows - 1 : rows]
        leave_row = factor[(f + 1) * rows - 1 : (f + 1) * rows] * last
        spread_row = jnp.sum(weighted[span] * factor[span, 0:1], axis=0, keepdims=True)
        leave = jnp.sum(jnp.where(lane == wide_row, leave_row, 0.0), axis=1, keepdims=True)
        spread = jnp.sum(jnp.where(lane == wide_row, spread_row, 0.0), axis=1, keepdims=True)
        coeffs = coeffs + jnp.where(coeff_lane == f, leave_row[:, 0:1], 0.0)
        coeffs = coeffs + jnp.where(coeff_lane == half + f, spread_row[:, 0:1], 0.0)
        here = place_field == f % pack
        line_through[f // pack] = jnp.where(here, leave_row[:, 0:1], line_through[f // pack])
        line_first[f // pack] = jnp.where(here, spread_row[:, 0:1], line_first[f // pack])
        spreads.append(jnp.broadcast_to(spread, (rows, length)))
        leaves.append(jnp.broadcast_to(leave, (rows, length)))
        speeds.append(jnp.broadcast_to(speed[span], (rows, length)))
        columns[0, f] = spreads[f][:, :128]
        columns[1, f] = leaves[f][:, :128]
        columns[2, f] = spreads[f][:, :128] * speeds[f][:, :128]
        columns[3, f] = leaves[f][:, :128] * speeds[f][:, :128]
    for o in range(n):
        sent[o, 2 * share : 2 * share + 1, :] = coeffs

    row_values[0] = jnp.broadcast_to(column(low_ref, 0), (total, 128))
    row_values[1] = jnp.broadcast_to(inverse_pivot, (total, 128))
    for load in loads:
        for part in load:
            part.wait()
    chains = [(f, h) for f in range(fields) for h in range(length // 128)]
    at = lambda f, h, j: (f, h, pl.ds(j, planes, stride=rows), slice(None))
    value = lambda i, f, j: row_values[i, f * rows + j : f * rows + j + 1, :]
    rising = [cot[at(f, h, 0)] for f, h in chains]
    scaled = [[rise * value(1, f, 0) for rise, (f, h) in zip(rising, chains)]]
    for j in range(1, rows):
        rising = [
            cot[at(f, h, j)] + value(0, f, j - 1) * rise for rise, (f, h) in zip(rising, chains)
        ]
        scaled.append([rise * value(1, f, j) for rise, (f, h) in zip(rising, chains)])
    lift = [value(0, f, rows - 1) * rise for rise, (f, h) in zip(rising, chains)]
    adjoint = scaled[rows - 1]
    for j in range(rows - 1, -1, -1):
        if j < rows - 1:
            adjoint = [
                part + value(0, f, j) * below
                for part, below, (f, h) in zip(scaled[j], adjoint, chains)
            ]
        for solved, (f, h) in zip(adjoint, chains):
            settle[at(f, h, j)] = solved
    for i, (f, h) in enumerate(chains):
        lane_span = slice(128 * h, 128 * (h + 1))
        z = 0
        while z < planes:
            o, up = divmod(f * planes + z, share)
            run = min(planes - z, share - up)
            sent[o, up : up + run, lane_span] = lift[i][z : z + run]
            sent[o, share + up : share + up + run, lane_span] = adjoint[i][z : z + run]
            z += run

    pl.semaphore_wait(barrier, n + 1)

    first = [swap(sent, got, send1, recv1, d) for d in range(1, n)]
    for copy in first:
        copy.start()
    got[wall] = sent[wall]

    def joined(ref, f):
        return jnp.concatenate([ref[f, h] for h in range(length // 128)], axis=1)

    wide_place = lax.broadcasted_iota(jnp.int32, (rows, 256), 1) % 128 // 2
    for g in range(groups):
        tile = jnp.zeros((rows, 256), jnp.float32)
        for f in range(g * pack, min(fields, (g + 1) * pack)):
            sums = through_stencil(joined(cot, f), weights)
            for z in range(planes):
                mine = wide_place == planes * (f % pack) + z
                tile = jnp.where(mine, sums[z * rows : (z + 1) * rows], tile)
        to_right[g] = tile[:, :128]
        to_left[g] = tile[:, 128:]
    edge_copies = beside(
        ((to_right, from_left, right), (to_left, from_right, left)), send3, recv3
    )
    for copy in edge_copies:
        copy.start()

    profile = edge_profiles(length)
    lane_at = lax.broadcasted_iota(jnp.int32, (128, length), 0)
    profile = jnp.concatenate(
        [
            jnp.where(lane_at % 2 == 0, profile[i : i + 1], profile[i + 1 : i + 2])
            for i in (0, 2)
        ],
        axis=0,
    )
    high = profile.astype(jnp.bfloat16).astype(jnp.float32)
    rest = profile - high
    slot = lax.broadcasted_iota(jnp.int32, (256, length), 0) % 128 // (2 * planes)
    mixed = jnp.where(slot < 2, high, jnp.where(slot == 2, rest, 0.0))
    profiles[0] = high.astype(jnp.bfloat16)
    profiles[1] = rest.astype(jnp.bfloat16)
    profiles[2] = mixed.astype(jnp.bfloat16)

    operators = []

    def row_operator(f):
        span = slice(f * rows, (f + 1) * rows)
        gram = lax.dot_general(
            weighted[span], factor[span], (((0,), (0,)), ((), ())),
            precision=lax.Precision.HIGHEST, preferred_element_type=jnp.float32,
        )[:rows]
        high = gram.astype(jnp.bfloat16).astype(jnp.float32)
        operator = jnp.where(lane < 2 * rows, high, gram - high).astype(jnp.bfloat16)
        operators.append(operator)

    for f in range(fields):
        row_operator(f)
    for d in range(1, n):
        arrive(sent, got, send1, recv1, d)

    share_field = (wall * share + lax.broadcasted_iota(jnp.int32, (share, length), 0)) // planes
    share_lane = lax.broadcasted_iota(jnp.int32, (share, length), 1)
    incoming = jnp.zeros((share, length), jnp.float32)
    through, crest = [], []
    for b in range(n):
        coeff_row = got[b, 2 * share : 2 * share + 1, :]
        t = jnp.sum(jnp.where(share_lane == share_field, coeff_row, 0.0), axis=1, keepdims=True)
        p = jnp.sum(
            jnp.where(share_lane == share_field + half, coeff_row, 0.0), axis=1, keepdims=True
        )
        answer[b, 0:share, :] = incoming
        through.append(t)
        crest.append(got[b, share : 2 * share, :] + p * incoming)
        incoming = t * incoming + got[b, 0:share, :]
    descent = jnp.zeros((share, length), jnp.float32)
    for b in range(n - 1, -1, -1):
        answer[b, share : 2 * share, :] = descent
        answer[b, 2 * share :, :] = jnp.zeros((depth - 2 * share, length), jnp.float32)
        descent = through[b] * descent + crest[b]

    second = [swap(answer, carried, send2, recv2, d) for d in range(1, n)]
    for copy in second:
        copy.start()
    carried[wall] = answer[wall]

    for copy in edge_copies:
        copy.wait_recv()
    beyond = [jnp.concatenate([from_left[g], from_right[g]], axis=1) for g in range(groups)]
    for g in range(groups):
        lift = jnp.zeros((1, 256), jnp.float32)
        drop = lift
        for f in range(g * pack, min(fields, (g + 1) * pack)):
            here = place_field == f % pack
            leave, spread = leaves[f][:, :1], spreads[f][:, :1]
            lift = jnp.where(here, jnp.sum(leave * beyond[g], axis=0, keepdims=True), lift)
            drop = jnp.where(here, jnp.sum(spread * beyond[g], axis=0, keepdims=True), drop)
        ends[g : g + 1, :] = lift
        ends[groups + g : groups + g + 1, :] = drop
        ends[2 * groups + g : 2 * groups + g + 1, :] = line_through[g]
        ends[3 * groups + g : 3 * groups + g + 1, :] = line_first[g]
    if ends.shape[0] > 4 * groups:
        ends[4 * groups :, :] = jnp.zeros((ends.shape[0] - 4 * groups, 256), jnp.float32)
    gather = [
        pltpu.make_async_remote_copy(
            src_ref=ends, dst_ref=ends_got.at[wall],
            send_sem=send4.at[lax.rem(wall + d, n)], recv_sem=recv4.at[wall],
            device_id={"wall": lax.rem(wall + d, n)}, device_id_type=MESH,
        )
        for d in range(1, n)
    ]
    for copy in gather:
        copy.start()
    ends_got[wall] = ends[...]

    width = 2 * planes
    narrow = lax.broadcasted_iota(jnp.int32, (rows, 128), 1)
    wide_plane = lax.broadcasted_iota(jnp.int32, (rows, 256), 1) % width // 2
    for f in range(fields):
        solved = joined(settle, f)
        solved = solved.reshape(planes, rows, length)
        flux = (solved * speeds[f]).reshape(planes * rows, length)
        slope = through_stencil(flux, stencil)
        sums = jnp.dot(
            operators[f], stacked_both(beyond[f // pack]), preferred_element_type=jnp.float32
        )
        sides = []
        for i in range(2):
            part = speeds[f][:, :128] * sums[:, 128 * i : 128 * (i + 1)]
            if f % pack:
                part = pltpu.roll(part, 128 - width * (f % pack), 1)
            part = jnp.where(narrow < width, part, 0.0)
            high = part.astype(jnp.bfloat16).astype(jnp.float32)
            sides.append(
                high + pltpu.roll(part - high, width, 1) + pltpu.roll(high, 2 * width, 1)
            )
        side = jnp.concatenate(sides, axis=1)
        spaced = jnp.concatenate(
            [jnp.where(wide_plane == z, side, 0.0) for z in range(planes)], axis=0
        )
        slope = slope + jnp.dot(
            spaced.astype(jnp.bfloat16), profiles[2], preferred_element_type=jnp.float32
        )
        base[f] = solved + slope.reshape(planes, rows, length)

    for d in range(1, n):
        peer = lax.rem(wall + d, n)
        pltpu.make_async_remote_copy(
            src_ref=ends, dst_ref=ends_got.at[peer],
            send_sem=send4.at[peer], recv_sem=recv4.at[peer],
            device_id={"wall": peer}, device_id_type=MESH,
        ).wait_recv()
    zero = jnp.zeros((groups, 256), jnp.float32)
    incoming, taken_up, through, crest = zero, zero, [], []
    for b in range(n):
        lift, drop, t, p = (ends_got[b, i * groups : (i + 1) * groups, :] for i in range(4))
        taken_up = jnp.where(wall == b, incoming, taken_up)
        through.append(t)
        crest.append(drop + p * incoming)
        incoming = t * incoming + lift
    descent, taken_down = zero, zero
    for b in range(n - 1, -1, -1):
        taken_down = jnp.where(wall == b, descent, taken_down)
        descent = through[b] * descent + crest[b]
    line_sums[...] = jnp.zeros(line_sums.shape, jnp.float32)
    for line in range(fields * planes):
        f, z = line // planes, line % planes
        g, o, up = f // pack, line // share, line % share
        mine = place // 2 == planes * (f % pack) + z
        line_sums[o, up : up + 1, :] = jnp.where(mine, taken_up[g : g + 1], 0.0)
        line_sums[o, share + up : share + up + 1, :] = jnp.where(mine, taken_down[g : g + 1], 0.0)
    halo = through_stencil(line_sums[...].reshape(n * depth, 256), profiles)

    for d in range(1, n):
        arrive(answer, carried, send2, recv2, d)
    flat = carried[...].reshape(n * depth, length)
    slope = through_stencil(flat, stencil) + halo
    carried_out[...] = carried[...]
    slope_out[...] = slope.reshape(n, depth, length)

    for copy in first + second + gather + edge_copies:
        copy.wait_send()


def gather_kernel(
    fields, planes, rows, length, share, base, carried, slopes, columns, out_hbm, out, store_sem
):
    stores = []
    for f in range(fields):
        spread, leave, spread_speed, leave_speed = (
            jnp.concatenate([columns[i, f]] * (length // 128), axis=1) for i in range(4)
        )
        for z in range(planes):
            line = f * planes + z
            o, up = line // share, line % share
            low = share + up
            value = base[f, z] + spread * carried[o, up : up + 1, :]
            value = value + leave * carried[o, low : low + 1, :]
            value = value + spread_speed * slopes[o, up : up + 1, :]
            out[f, z] = value + leave_speed * slopes[o, low : low + 1, :]
        store = pltpu.make_async_copy(out.at[f], out_hbm.at[f], store_sem.at[f])
        store.start()
        stores.append(store)
    for store in stores:
        store.wait()


def local(n, streams, cotangent, lower, pivot, speed):
    fields, planes, rows, length = cotangent.shape
    share = -(-fields * planes // n)
    depth = up_to(2 * share + 1, 8)
    pack = 128 // (2 * planes)
    groups = -(-fields // pack)
    end_rows = up_to(4 * groups, 8)
    edge_shape = (groups, rows, 128)
    line_shape = (n, depth, length)
    column_shape = (4, fields, rows, 128)
    vmem = pl.BlockSpec(memory_space=pltpu.VMEM)
    hbm = pl.BlockSpec(memory_space=pltpu.HBM)
    f32 = jnp.float32
    dma = pltpu.SemaphoreType.DMA
    scratch = lambda shape: pltpu.VMEM(shape, f32)
    out_shapes = (cotangent.shape, line_shape, line_shape, column_shape)
    parts = pl.pallas_call(
        functools.partial(
            exchange_kernel, n, streams, fields, planes, rows, length, share, depth, pack
        ),
        out_shape=tuple(jax.ShapeDtypeStruct(shape, f32) for shape in out_shapes),
        in_specs=[hbm] * 4,
        out_specs=(vmem,) * 4,
        scratch_shapes=[scratch((fields, length // 128, planes * rows, 128))] * 2
        + [scratch((2, fields * rows, 128))]
        + [scratch(lower.shape)] * 3
        + [scratch(line_shape)] * 4
        + [scratch((end_rows, 256)), scratch((n, end_rows, 256)), scratch((n, depth, 256))]
        + [scratch(edge_shape)] * 4
        + [pltpu.VMEM((2, length, length), jnp.bfloat16)]
        + [pltpu.VMEM((2, length, 256), jnp.bfloat16)]
        + [pltpu.VMEM((3, 256, length), jnp.bfloat16)]
        + [dma((fields, length // 128)), dma((3,))]
        + [dma((n,))] * 4
        + [dma((2,))] * 2
        + [dma((n,))] * 2,
        compiler_params=pltpu.CompilerParams(
            collective_id=0, has_side_effects=True, vmem_limit_bytes=VMEM_LIMIT
        ),
    )(*[
        pltpu.with_memory_space_constraint(a, pltpu.HBM)
        for a in (cotangent.reshape(fields, planes * rows, length), lower, pivot, speed)
    ])
    return pl.pallas_call(
        functools.partial(gather_kernel, fields, planes, rows, length, share),
        out_shape=jax.ShapeDtypeStruct(cotangent.shape, f32),
        in_specs=[vmem] * 4,
        out_specs=hbm,
        scratch_shapes=[scratch(cotangent.shape), dma((fields,))],
        compiler_params=pltpu.CompilerParams(vmem_limit_bytes=VMEM_LIMIT),
    )(*parts)


def solution(mesh):
    return jax.shard_map(
        functools.partial(local, mesh.shape["wall"], mesh.shape["stream"]),
        mesh=mesh,
        in_specs=(
            P(None, None, "wall", "stream"),
            P(None, "wall"),
            P(None, "wall"),
            P(None, "wall"),
        ),
        out_specs=P(None, None, "wall", "stream"),
        check_vma=False,
    )
```

```python
import functools
import math

import jax
import jax.numpy as jnp
from jax import lax
from jax.experimental import pallas as pl
from jax.experimental.pallas import tpu as pltpu
from jax.sharding import PartitionSpec as P

root_value = (math.sqrt(5.0) - 3.0) / 2.0
inverse_gain = 3.0 / math.sqrt(5.0)
first_coeff = 7.0 / 9.0
second_coeff = 1.0 / 36.0
MESH = pl.DeviceIdType.MESH
VMEM_LIMIT = 40 * 1024 * 1024


def up_to(value, unit):
    return -(-value // unit) * unit


def split(values):
    high = values.astype(jnp.bfloat16)
    low = (values - high.astype(jnp.float32)).astype(jnp.bfloat16)
    return high, low


def root_power(steps):
    even = steps - 2.0 * jnp.floor(steps * 0.5) == 0.0
    size = jnp.exp(steps * math.log(-root_value))
    return jnp.where(even, size, -size)


far_scale = inverse_gain * (
    first_coeff * (1.0 / root_value - root_value)
    + second_coeff * (root_value**-2 - root_value**2)
)
near_shift = inverse_gain * second_coeff * (root_value - 1.0 / root_value)


def stencil_block(length):
    source = lax.broadcasted_iota(jnp.int32, (length, length), 0)
    target = lax.broadcasted_iota(jnp.int32, (length, length), 1)
    offset = source - target
    steps = jnp.abs(offset).astype(jnp.float32)
    size = far_scale * root_power(steps) + jnp.where(steps == 1.0, near_shift, 0.0)
    return jnp.where(offset > 0, size, jnp.where(offset < 0, -size, 0.0))


def edge_weights(length):
    cell = lax.broadcasted_iota(jnp.int32, (length, 128), 0)
    odd = lax.broadcasted_iota(jnp.int32, (length, 128), 1) % 2 == 1
    sides = []
    for depth in (length - 1 - cell, cell):
        edge = jnp.where(depth == 0, 1.0, 0.0)
        sides.append(jnp.where(odd, edge, root_power(depth.astype(jnp.float32))))
    return jnp.concatenate(sides, axis=1)


def edge_profiles(length):
    row = lax.broadcasted_iota(jnp.int32, (8, length), 0)
    cell = lax.broadcasted_iota(jnp.int32, (8, length), 1)
    back = length - 1 - cell
    depth = jnp.where(row < 2, cell, back)
    decay = far_scale * root_power((depth + 1).astype(jnp.float32))
    edge = jnp.where(depth == 0, near_shift, 0.0)
    profile = jnp.where((row == 0) | (row == 2), decay, edge)
    return jnp.where(row < 2, -profile, jnp.where(row < 4, profile, 0.0))


def stacked_both(values):
    high, low = split(values)
    return jnp.concatenate([high, low, high, low], axis=0)


def through_stencil(values, stencil):
    high, low = split(values)
    slope = jnp.dot(high, stencil[0], preferred_element_type=jnp.float32)
    slope = slope + jnp.dot(low, stencil[0], preferred_element_type=jnp.float32)
    return slope + jnp.dot(high, stencil[1], preferred_element_type=jnp.float32)


def exchange_kernel(
    n, streams, fields, planes, rows, length, share, depth, pack,
    cot_hbm, low_hbm, pivot_hbm, speed_hbm,
    base, carried_out, slope_out, columns,
    cot, low_ref, pivot_ref, speed_ref, sent, got, answer, carried,
    ends, ends_got, line_sums, to_left, to_right, from_left, from_right, stencil, weights, profiles,
    load_sem, row_sem, send1, recv1, send2, recv2, send3, recv3, send4, recv4,
):
    wall = lax.axis_index("wall")
    stream = lax.axis_index("stream")
    right = lax.rem(stream + 1, streams)
    left = lax.rem(stream + streams - 1, streams)

    row_loads = [
        pltpu.make_async_copy(source, target, row_sem.at[i])
        for i, (source, target) in enumerate(
            ((low_hbm, low_ref), (pivot_hbm, pivot_ref), (speed_hbm, speed_ref))
        )
    ]
    for load in row_loads:
        load.start()
    loads = [
        pltpu.make_async_copy(cot_hbm.at[f], cot.at[f], load_sem.at[f]) for f in range(fields)
    ]
    for load in loads:
        load.start()

    barrier = pltpu.get_barrier_semaphore()
    for d in range(1, n):
        pl.semaphore_signal(
            barrier, inc=1, device_id={"wall": lax.rem(wall + d, n)}, device_id_type=MESH
        )
    for side in (left, right):
        pl.semaphore_signal(barrier, inc=1, device_id={"stream": side}, device_id_type=MESH)

    def swap(source, target, send, recv, d):
        peer = lax.rem(wall + d, n)
        return pltpu.make_async_remote_copy(
            src_ref=source.at[peer], dst_ref=target.at[wall],
            send_sem=send.at[peer], recv_sem=recv.at[wall],
            device_id={"wall": peer}, device_id_type=MESH,
        )

    def arrive(source, target, send, recv, d):
        peer = lax.rem(wall + d, n)
        pltpu.make_async_remote_copy(
            src_ref=source.at[peer], dst_ref=target.at[peer],
            send_sem=send.at[peer], recv_sem=recv.at[peer],
            device_id={"wall": peer}, device_id_type=MESH,
        ).wait_recv()

    def beside(pairs, send, recv):
        return [
            pltpu.make_async_remote_copy(
                src_ref=source, dst_ref=target, send_sem=send.at[i], recv_sem=recv.at[i],
                device_id={"stream": side}, device_id_type=MESH,
            )
            for i, (source, target, side) in enumerate(pairs)
        ]

    sent[...] = jnp.zeros(sent.shape, jnp.float32)
    for i, part in enumerate(split(edge_weights(length))):
        weights[i] = part
    for i, part in enumerate(split(stencil_block(length))):
        stencil[i] = part

    lanes = 4 * rows
    total = fields * rows
    row_at = lax.rem(lax.broadcasted_iota(jnp.int32, (total, lanes), 0), rows)
    col_at = lax.rem(lax.broadcasted_iota(jnp.int32, (total, lanes), 1), rows)
    small_row = lax.broadcasted_iota(jnp.int32, (rows, rows), 0)
    small_col = lax.broadcasted_iota(jnp.int32, (rows, rows), 1)

    def column(ref, shift):
        pick = small_row == small_col + shift
        return jnp.concatenate(
            [
                jnp.sum(jnp.where(pick, ref[f : f + 1, :], 0.0), axis=1, keepdims=True)
                for f in range(fields)
            ],
            axis=0,
        )

    for load in row_loads:
        load.wait()
    before = column(low_ref, 1)
    inverse_pivot = 1.0 / column(pivot_ref, 0)
    speed = column(speed_ref, 0)
    product = jnp.where(row_at > col_at, before, 1.0)
    step = 1
    while step < rows:
        product = product * jnp.where(row_at >= step, pltpu.roll(product, step, 0), 1.0)
        step *= 2
    factor = jnp.where(row_at >= col_at, product, 0.0)
    weighted = factor * inverse_pivot

    lane = lax.broadcasted_iota(jnp.int32, (rows, lanes), 1)
    wide_row = lax.broadcasted_iota(jnp.int32, (rows, lanes), 0)
    coeff_lane = lax.broadcasted_iota(jnp.int32, (1, length), 1)
    groups = -(-fields // pack)
    place = lax.broadcasted_iota(jnp.int32, (1, 256), 1) % 128
    place_field = place // (2 * planes)
    half = length // 2
    spreads, leaves, speeds = [], [], []
    coeffs = jnp.zeros((1, length), jnp.float32)
    line_through = [jnp.zeros((1, 256), jnp.float32)] * groups
    line_first = [jnp.zeros((1, 256), jnp.float32)] * groups
    for f in range(fields):
        span = slice(f * rows, (f + 1) * rows)
        last = low_ref[f : f + 1, rows - 1 : rows]
        leave_row = factor[(f + 1) * rows - 1 : (f + 1) * rows] * last
        spread_row = jnp.sum(weighted[span] * factor[span, 0:1], axis=0, keepdims=True)
        leave = jnp.sum(jnp.where(lane == wide_row, leave_row, 0.0), axis=1, keepdims=True)
        spread = jnp.sum(jnp.where(lane == wide_row, spread_row, 0.0), axis=1, keepdims=True)
        coeffs = coeffs + jnp.where(coeff_lane == f, leave_row[:, 0:1], 0.0)
        coeffs = coeffs + jnp.where(coeff_lane == half + f, spread_row[:, 0:1], 0.0)
        here = place_field == f % pack
        line_through[f // pack] = jnp.where(here, leave_row[:, 0:1], line_through[f // pack])
        line_first[f // pack] = jnp.where(here, spread_row[:, 0:1], line_first[f // pack])
        spreads.append(jnp.broadcast_to(spread, (rows, length)))
        leaves.append(jnp.broadcast_to(leave, (rows, length)))
        speeds.append(jnp.broadcast_to(speed[span], (rows, length)))
        columns[0, f] = spreads[f][:, :128]
        columns[1, f] = leaves[f][:, :128]
        columns[2, f] = spreads[f][:, :128] * speeds[f][:, :128]
        columns[3, f] = leaves[f][:, :128] * speeds[f][:, :128]
    for o in range(n):
        sent[o, 2 * share : 2 * share + 1, :] = coeffs

    for f in range(fields):
        loads[f].wait()
        for z in range(planes):
            line = f * planes + z
            values = cot[f, z]
            sent[line // share, line % share, :] = jnp.sum(values * leaves[f], axis=0)
            sent[line // share, share + line % share, :] = jnp.sum(values * spreads[f], axis=0)

    pl.semaphore_wait(barrier, n + 1)

    first = [swap(sent, got, send1, recv1, d) for d in range(1, n)]
    for copy in first:
        copy.start()
    got[wall] = sent[wall]

    wide_place = lax.broadcasted_iota(jnp.int32, (rows, 256), 1) % 128 // 2
    for g in range(groups):
        tile = jnp.zeros((rows, 256), jnp.float32)
        for f in range(g * pack, min(fields, (g + 1) * pack)):
            sums = through_stencil(cot[f].reshape(planes * rows, length), weights)
            for z in range(planes):
                mine = wide_place == planes * (f % pack) + z
                tile = jnp.where(mine, sums[z * rows : (z + 1) * rows], tile)
        to_right[g] = tile[:, :128]
        to_left[g] = tile[:, 128:]
    edge_copies = beside(
        ((to_right, from_left, right), (to_left, from_right, left)), send3, recv3
    )
    for copy in edge_copies:
        copy.start()

    profile = edge_profiles(length)
    lane_at = lax.broadcasted_iota(jnp.int32, (128, length), 0)
    profile = jnp.concatenate(
        [
            jnp.where(lane_at % 2 == 0, profile[i : i + 1], profile[i + 1 : i + 2])
            for i in (0, 2)
        ],
        axis=0,
    )
    high = profile.astype(jnp.bfloat16).astype(jnp.float32)
    rest = profile - high
    slot = lax.broadcasted_iota(jnp.int32, (256, length), 0) % 128 // (2 * planes)
    mixed = jnp.where(slot < 2, high, jnp.where(slot == 2, rest, 0.0))
    profiles[0] = high.astype(jnp.bfloat16)
    profiles[1] = rest.astype(jnp.bfloat16)
    profiles[2] = mixed.astype(jnp.bfloat16)

    operators = []

    def settle_field(f):
        span = slice(f * rows, (f + 1) * rows)
        gram = lax.dot_general(
            weighted[span], factor[span], (((0,), (0,)), ((), ())),
            precision=lax.Precision.HIGHEST, preferred_element_type=jnp.float32,
        )[:rows]
        high = gram.astype(jnp.bfloat16).astype(jnp.float32)
        operator = jnp.where(lane < 2 * rows, high, gram - high).astype(jnp.bfloat16)
        operators.append(operator)
        for z in range(planes):
            high, low = split(cot[f, z])
            out = jnp.dot(
                operator,
                jnp.concatenate([high, low, high, low], axis=0),
                preferred_element_type=jnp.float32,
            )
            base[f, z] = out
            cot[f, z] = speeds[f] * out

    early = (fields + 1) // 2
    for f in range(early):
        settle_field(f)
    for d in range(1, n):
        arrive(sent, got, send1, recv1, d)

    share_field = (wall * share + lax.broadcasted_iota(jnp.int32, (share, length), 0)) // planes
    share_lane = lax.broadcasted_iota(jnp.int32, (share, length), 1)
    incoming = jnp.zeros((share, length), jnp.float32)
    through, crest = [], []
    for b in range(n):
        coeff_row = got[b, 2 * share : 2 * share + 1, :]
        t = jnp.sum(jnp.where(share_lane == share_field, coeff_row, 0.0), axis=1, keepdims=True)
        p = jnp.sum(
            jnp.where(share_lane == share_field + half, coeff_row, 0.0), axis=1, keepdims=True
        )
        answer[b, 0:share, :] = incoming
        through.append(t)
        crest.append(got[b, share : 2 * share, :] + p * incoming)
        incoming = t * incoming + got[b, 0:share, :]
    descent = jnp.zeros((share, length), jnp.float32)
    for b in range(n - 1, -1, -1):
        answer[b, share : 2 * share, :] = descent
        answer[b, 2 * share :, :] = jnp.zeros((depth - 2 * share, length), jnp.float32)
        descent = through[b] * descent + crest[b]

    second = [swap(answer, carried, send2, recv2, d) for d in range(1, n)]
    for copy in second:
        copy.start()
    carried[wall] = answer[wall]

    for copy in edge_copies:
        copy.wait_recv()
    beyond = [jnp.concatenate([from_left[g], from_right[g]], axis=1) for g in range(groups)]
    for g in range(groups):
        lift = jnp.zeros((1, 256), jnp.float32)
        drop = lift
        for f in range(g * pack, min(fields, (g + 1) * pack)):
            here = place_field == f % pack
            leave, spread = leaves[f][:, :1], spreads[f][:, :1]
            lift = jnp.where(here, jnp.sum(leave * beyond[g], axis=0, keepdims=True), lift)
            drop = jnp.where(here, jnp.sum(spread * beyond[g], axis=0, keepdims=True), drop)
        ends[g : g + 1, :] = lift
        ends[groups + g : groups + g + 1, :] = drop
        ends[2 * groups + g : 2 * groups + g + 1, :] = line_through[g]
        ends[3 * groups + g : 3 * groups + g + 1, :] = line_first[g]
    if ends.shape[0] > 4 * groups:
        ends[4 * groups :, :] = jnp.zeros((ends.shape[0] - 4 * groups, 256), jnp.float32)
    gather = [
        pltpu.make_async_remote_copy(
            src_ref=ends, dst_ref=ends_got.at[wall],
            send_sem=send4.at[lax.rem(wall + d, n)], recv_sem=recv4.at[wall],
            device_id={"wall": lax.rem(wall + d, n)}, device_id_type=MESH,
        )
        for d in range(1, n)
    ]
    for copy in gather:
        copy.start()
    ends_got[wall] = ends[...]

    for f in range(early, fields):
        settle_field(f)
    width = 2 * planes
    narrow = lax.broadcasted_iota(jnp.int32, (rows, 128), 1)
    wide_plane = lax.broadcasted_iota(jnp.int32, (rows, 256), 1) % width // 2
    for f in range(fields):
        slope = through_stencil(cot[f].reshape(planes * rows, length), stencil)
        sums = jnp.dot(
            operators[f], stacked_both(beyond[f // pack]), preferred_element_type=jnp.float32
        )
        sides = []
        for i in range(2):
            part = speeds[f][:, :128] * sums[:, 128 * i : 128 * (i + 1)]
            if f % pack:
                part = pltpu.roll(part, 128 - width * (f % pack), 1)
            part = jnp.where(narrow < width, part, 0.0)
            high = part.astype(jnp.bfloat16).astype(jnp.float32)
            sides.append(
                high + pltpu.roll(part - high, width, 1) + pltpu.roll(high, 2 * width, 1)
            )
        side = jnp.concatenate(sides, axis=1)
        spaced = jnp.concatenate(
            [jnp.where(wide_plane == z, side, 0.0) for z in range(planes)], axis=0
        )
        slope = slope + jnp.dot(
            spaced.astype(jnp.bfloat16), profiles[2], preferred_element_type=jnp.float32
        )
        base[f] = base[f] + slope.reshape(planes, rows, length)

    for d in range(1, n):
        peer = lax.rem(wall + d, n)
        pltpu.make_async_remote_copy(
            src_ref=ends, dst_ref=ends_got.at[peer],
            send_sem=send4.at[peer], recv_sem=recv4.at[peer],
            device_id={"wall": peer}, device_id_type=MESH,
        ).wait_recv()
    zero = jnp.zeros((groups, 256), jnp.float32)
    incoming, taken_up, through, crest = zero, zero, [], []
    for b in range(n):
        lift, drop, t, p = (ends_got[b, i * groups : (i + 1) * groups, :] for i in range(4))
        taken_up = jnp.where(wall == b, incoming, taken_up)
        through.append(t)
        crest.append(drop + p * incoming)
        incoming = t * incoming + lift
    descent, taken_down = zero, zero
    for b in range(n - 1, -1, -1):
        taken_down = jnp.where(wall == b, descent, taken_down)
        descent = through[b] * descent + crest[b]
    line_sums[...] = jnp.zeros(line_sums.shape, jnp.float32)
    for line in range(fields * planes):
        f, z = line // planes, line % planes
        g, o, up = f // pack, line // share, line % share
        mine = place // 2 == planes * (f % pack) + z
        line_sums[o, up : up + 1, :] = jnp.where(mine, taken_up[g : g + 1], 0.0)
        line_sums[o, share + up : share + up + 1, :] = jnp.where(mine, taken_down[g : g + 1], 0.0)
    halo = through_stencil(line_sums[...].reshape(n * depth, 256), profiles)

    for d in range(1, n):
        arrive(answer, carried, send2, recv2, d)
    flat = carried[...].reshape(n * depth, length)
    slope = through_stencil(flat, stencil) + halo
    carried_out[...] = carried[...]
    slope_out[...] = slope.reshape(n, depth, length)

    for copy in first + second + gather + edge_copies:
        copy.wait_send()


def gather_kernel(
    fields, planes, rows, length, share, base, carried, slopes, columns, out_hbm, out, store_sem
):
    stores = []
    for f in range(fields):
        spread, leave, spread_speed, leave_speed = (
            jnp.concatenate([columns[i, f]] * (length // 128), axis=1) for i in range(4)
        )
        for z in range(planes):
            line = f * planes + z
            o, up = line // share, line % share
            low = share + up
            value = base[f, z] + spread * carried[o, up : up + 1, :]
            value = value + leave * carried[o, low : low + 1, :]
            value = value + spread_speed * slopes[o, up : up + 1, :]
            out[f, z] = value + leave_speed * slopes[o, low : low + 1, :]
        store = pltpu.make_async_copy(out.at[f], out_hbm.at[f], store_sem.at[f])
        store.start()
        stores.append(store)
    for store in stores:
        store.wait()


def local(n, streams, cotangent, lower, pivot, speed):
    fields, planes, rows, length = cotangent.shape
    share = -(-fields * planes // n)
    depth = up_to(2 * share + 1, 8)
    pack = 128 // (2 * planes)
    groups = -(-fields // pack)
    end_rows = up_to(4 * groups, 8)
    edge_shape = (groups, rows, 128)
    line_shape = (n, depth, length)
    column_shape = (4, fields, rows, 128)
    vmem = pl.BlockSpec(memory_space=pltpu.VMEM)
    hbm = pl.BlockSpec(memory_space=pltpu.HBM)
    f32 = jnp.float32
    dma = pltpu.SemaphoreType.DMA
    scratch = lambda shape: pltpu.VMEM(shape, f32)
    out_shapes = (cotangent.shape, line_shape, line_shape, column_shape)
    parts = pl.pallas_call(
        functools.partial(
            exchange_kernel, n, streams, fields, planes, rows, length, share, depth, pack
        ),
        out_shape=tuple(jax.ShapeDtypeStruct(shape, f32) for shape in out_shapes),
        in_specs=[hbm] * 4,
        out_specs=(vmem,) * 4,
        scratch_shapes=[scratch(cotangent.shape)]
        + [scratch(lower.shape)] * 3
        + [scratch(line_shape)] * 4
        + [scratch((end_rows, 256)), scratch((n, end_rows, 256)), scratch((n, depth, 256))]
        + [scratch(edge_shape)] * 4
        + [pltpu.VMEM((2, length, length), jnp.bfloat16)]
        + [pltpu.VMEM((2, length, 256), jnp.bfloat16)]
        + [pltpu.VMEM((3, 256, length), jnp.bfloat16)]
        + [dma((fields,)), dma((3,))]
        + [dma((n,))] * 4
        + [dma((2,))] * 2
        + [dma((n,))] * 2,
        compiler_params=pltpu.CompilerParams(
            collective_id=0, has_side_effects=True, vmem_limit_bytes=VMEM_LIMIT
        ),
    )(*[
        pltpu.with_memory_space_constraint(a, pltpu.HBM)
        for a in (cotangent, lower, pivot, speed)
    ])
    return pl.pallas_call(
        functools.partial(gather_kernel, fields, planes, rows, length, share),
        out_shape=jax.ShapeDtypeStruct(cotangent.shape, f32),
        in_specs=[vmem] * 4,
        out_specs=hbm,
        scratch_shapes=[scratch(cotangent.shape), dma((fields,))],
        compiler_params=pltpu.CompilerParams(vmem_limit_bytes=VMEM_LIMIT),
    )(*parts)


def solution(mesh):
    return jax.shard_map(
        functools.partial(local, mesh.shape["wall"], mesh.shape["stream"]),
        mesh=mesh,
        in_specs=(
            P(None, None, "wall", "stream"),
            P(None, "wall"),
            P(None, "wall"),
            P(None, "wall"),
        ),
        out_specs=P(None, None, "wall", "stream"),
        check_vma=False,
    )
```
